32 devices in a mesh: tm: 8 (over y, x, core), space: 4 (over z).
Axes of the slice: x: 2, y: 2, z: 4, core: 2. Of those that a mesh axis runs over, the one named last changes fastest.
Arguments:
- queries: bfloat16 [16, 32, 8, 1024], P('tm', None, 'space'), may hold values from -16 to 16
- key_rows: bfloat16 [16, 32, 8, 1024], P('tm', None, 'space'), may hold values from -6 to 6
- value_rows: bfloat16 [16, 32, 8, 1024], P('tm', None, 'space'), may hold values from -5 to 5
- out_proj: bfloat16 [1024, 512], replicated, may hold values from -0.1875 to 0.1875
- conv_taps: bfloat16 [3, 3, 3, 512, 512], replicated, may hold values from -0.0546875 to 0.0546875
- cotangent: bfloat16 [16, 32, 8, 512], P('tm', None, 'space'), may hold values from -6 to 6
Outputs:
- conv_output: bfloat16 [16, 32, 8, 512], P('tm', None, 'space')
- grad_queries: bfloat16 [16, 32, 8, 1024], P('tm', None, 'space')
- grad_keys: bfloat16 [16, 32, 8, 1024], P('tm', None, 'space')
- grad_values: bfloat16 [16, 32, 8, 1024], P('tm', None, 'space')
The draws below stay inside these ranges and needn't reach their ends.
All inputs are finite; a program needn't handle non-finite values.
Results may differ from the reference program's by a relative error of at most 0.019.
Values may be sent and summed in bfloat16 or wider, within the bound.
A program may use at most 128 MiB of HBM per device.

```python
import jax
import jax.numpy as jnp
from jax import lax

HEADS = 16
HEAD = 64
CH = 512
ROWS = 32
FRAMES = 16
COLS = 8


def attention_pair(key):
    base = jax.random.fold_in(key, 31)
    first_key, second_key = jax.random.split(base, 2)
    count = FRAMES * ROWS * COLS
    width = HEADS * HEAD
    query_new = jnp.clip(jax.random.normal(first_key, (count, width), jnp.float32), -4.0, 4.0)
    key_new = jnp.clip(jax.random.normal(second_key, (count, width), jnp.float32), -4.0, 4.0)
    return (query_new.reshape(FRAMES, ROWS, COLS, width), key_new.reshape(FRAMES, ROWS, COLS, width))


def draw_queries(key, part):
    return attention_pair(key)[0].astype(jnp.bfloat16)


def draw_key_rows(key, part):
    return attention_pair(key)[1].astype(jnp.bfloat16)


def steps_of(stream_key, shape, cuts, smallest, high):
    loudness, own = 1.0, jax.random.fold_in(stream_key, 6)
    for dim, blocks in cuts:
        heights = jnp.exp(jax.random.uniform(jax.random.fold_in(own, dim), (blocks,), jnp.float32, smallest / len(cuts), high / len(cuts)))
        loudness = loudness * jnp.repeat(heights, shape[dim] // blocks).reshape([-1 if axis == dim else 1 for axis in range(len(shape))])
    return loudness


def noise(own_key, shape, deviation, limit, cuts=(), kind=jnp.bfloat16):
    result = deviation * jax.random.normal(own_key, shape, jnp.float32)
    if cuts:
        result = result * steps_of(own_key, shape, cuts, -0.22, 0.18)
    return jnp.clip(result, -limit, limit).astype(kind)


def setup_inputs(seed: int = 0) -> dict:
    seeds = jax.random.split(jax.random.key(seed), 7)
    queries = draw_queries(jax.random.fold_in(seeds[6], 71), 0)
    key_rows = draw_key_rows(jax.random.fold_in(seeds[6], 71), 0)
    value_rows = noise(seeds[2], (FRAMES, ROWS, COLS, HEADS * HEAD), 1.0, 5.0, ((0, 8), (2, 4)))
    out_proj = noise(seeds[3], (HEADS * HEAD, CH), (HEADS * HEAD) ** -0.5, 0.1875)
    conv_taps = noise(seeds[4], (3, 3, 3, CH, CH), (27 * CH) ** -0.5, 0.0546875)
    cotangent = noise(seeds[5], (FRAMES, ROWS, COLS, CH), 1.0, 6.0, ((0, 8), (2, 4)))
    return {"queries": queries, "key_rows": key_rows, "value_rows": value_rows, "out_proj": out_proj, "conv_taps": conv_taps, "cotangent": cotangent}


HIGHEST = lax.Precision.HIGHEST


def heads_first(array):
    return array.reshape(FRAMES * ROWS * COLS, HEADS, HEAD).transpose(1, 0, 2)


def tokens_last(array):
    return array.transpose(1, 0, 2).reshape(FRAMES, ROWS, COLS, HEADS * HEAD)


def frozen(array):
    return lax.optimization_barrier(array.astype(jnp.bfloat16)).astype(jnp.float32)


def head_forward(operands):
    query_head = operands[0].astype(jnp.float32)
    key_head = operands[1].astype(jnp.float32)
    value_head = operands[2].astype(jnp.float32)
    scale = HEAD ** -0.5
    frame_tok = ROWS * COLS
    outputs = []
    logsums = []
    for frame in range(FRAMES):
        start = frame * frame_tok
        finish = start + frame_tok
        scores = jnp.dot(query_head[start:finish], key_head[:finish].T, precision=HIGHEST) * scale
        largest = jnp.max(scores, axis=1, keepdims=True)
        weights = jnp.exp(scores - largest)
        total = jnp.sum(weights, axis=1, keepdims=True)
        mixed = jnp.dot(frozen(weights), value_head[:finish], precision=HIGHEST) / total
        outputs.append(mixed.astype(jnp.bfloat16))
        logsums.append(largest[:, 0] + jnp.log(total[:, 0]))
    return jnp.concatenate(outputs, axis=0), jnp.concatenate(logsums, axis=0)


def head_backward(operands):
    query_head = operands[0].astype(jnp.float32)
    key_head = operands[1].astype(jnp.float32)
    value_head = operands[2].astype(jnp.float32)
    grad_head = operands[3].astype(jnp.float32)
    logsum = operands[4]
    delta = operands[5]
    scale = HEAD ** -0.5
    frame_tok = ROWS * COLS
    count = FRAMES * frame_tok
    query_parts = []
    grad_keys = jnp.zeros((count, HEAD), jnp.float32)
    grad_values = jnp.zeros((count, HEAD), jnp.float32)
    for frame in range(FRAMES):
        start = frame * frame_tok
        finish = start + frame_tok
        scores = jnp.dot(query_head[start:finish], key_head[:finish].T, precision=HIGHEST) * scale
        probs = jnp.exp(scores - logsum[start:finish, None])
        grad_values = grad_values.at[:finish].add(jnp.dot(frozen(probs).T, grad_head[start:finish], precision=HIGHEST))
        grad_probs = jnp.dot(grad_head[start:finish], value_head[:finish].T, precision=HIGHEST)
        grad_scores = frozen(probs * (grad_probs - delta[start:finish, None]))
        query_parts.append(jnp.dot(grad_scores, key_head[:finish], precision=HIGHEST) * scale)
        grad_keys = grad_keys.at[:finish].add(jnp.dot(grad_scores.T, query_head[start:finish], precision=HIGHEST) * scale)
    return jnp.concatenate(query_parts, axis=0), grad_keys, grad_values


def wrap_columns(padded):
    return jnp.concatenate([padded[:, :, -1:], padded, padded[:, :, :1]], axis=2)


def causal_conv(field, taps):
    padded = wrap_columns(jnp.pad(field, ((2, 0), (1, 1), (0, 0), (0, 0))))
    total = jnp.zeros((FRAMES * ROWS * COLS, CH), jnp.float32)
    for lag in range(3):
        for row_step in range(3):
            for col_step in range(3):
                window = padded[lag:lag + FRAMES, row_step:row_step + ROWS, col_step:col_step + COLS].reshape(-1, CH)
                total = total + jnp.dot(window, taps[lag, row_step, col_step], precision=HIGHEST)
    return total


def causal_conv_adjoint(field, taps):
    padded = wrap_columns(jnp.pad(field, ((0, 2), (1, 1), (0, 0), (0, 0))))
    total = jnp.zeros((FRAMES * ROWS * COLS, CH), jnp.float32)
    for lag in range(3):
        for row_step in range(3):
            for col_step in range(3):
                window = padded[2 - lag:2 - lag + FRAMES, 2 - row_step:2 - row_step + ROWS, 2 - col_step:2 - col_step + COLS].reshape(-1, CH)
                total = total + jnp.dot(window, taps[lag, row_step, col_step].T, precision=HIGHEST)
    return total


def reference(queries, key_rows, value_rows, out_proj, conv_taps, cotangent):
    query_heads = heads_first(queries)
    key_heads = heads_first(key_rows)
    value_heads = heads_first(value_rows)
    attended, logsums = lax.map(head_forward, (query_heads, key_heads, value_heads))
    attended_tokens = tokens_last(attended)
    projected = jnp.dot(attended_tokens.reshape(-1, HEADS * HEAD), out_proj, preferred_element_type=jnp.float32).astype(jnp.bfloat16)
    taps_wide = conv_taps.astype(jnp.float32)
    projected_wide = projected.astype(jnp.float32)
    mixed = causal_conv(projected_wide.reshape(FRAMES, ROWS, COLS, CH), taps_wide)
    conv_output = (projected_wide + mixed).astype(jnp.bfloat16).reshape(FRAMES, ROWS, COLS, CH)
    cot_wide = cotangent.astype(jnp.float32)
    grad_projected = (cot_wide.reshape(-1, CH) + causal_conv_adjoint(cot_wide, taps_wide)).astype(jnp.bfloat16)
    grad_attended = jnp.dot(grad_projected, out_proj.T, preferred_element_type=jnp.float32).astype(jnp.bfloat16)
    grad_heads = heads_first(grad_attended.reshape(FRAMES, ROWS, COLS, HEADS * HEAD))
    deltas = jnp.sum(grad_heads.astype(jnp.float32) * attended.astype(jnp.float32), axis=2)
    grad_q, grad_k, grad_v = lax.map(head_backward, (query_heads, key_heads, value_heads, grad_heads, logsums, deltas))
    return (conv_output,
            tokens_last(grad_q.astype(jnp.bfloat16)),
            tokens_last(grad_k.astype(jnp.bfloat16)),
            tokens_last(grad_v.astype(jnp.bfloat16)))
```

```python
import functools

import jax
import jax.numpy as jnp
from jax import lax
from jax.experimental import pallas as pl
from jax.experimental.pallas import tpu as pltpu
from jax.sharding import PartitionSpec as P

HEAD = 64
NEGATIVE = -1e30
F32 = jnp.float32
BF16 = jnp.bfloat16
VMEM = pl.BlockSpec(memory_space=pltpu.VMEM)


def dot(left, right):
    return jnp.dot(left, right, preferred_element_type=F32)


def attention_kernel(
    frames, frame_part, scale, qg_ref, kv_ref, oq_ref, dkv_ref, weights, scores, kv_turned
):
    blocks, q_tok, lanes = qg_ref.shape
    k_tok = kv_ref.shape[1]
    upper = lax.broadcasted_iota(jnp.int32, (lanes, q_tok), 0) < HEAD
    key_frame = lax.broadcasted_iota(jnp.int32, (k_tok, q_tok), 0) // frame_part % frames
    query_frame = lax.broadcasted_iota(jnp.int32, (k_tok, q_tok), 1) // frame_part % frames
    visible = key_frame <= query_frame

    @pl.loop(0, blocks)
    def _(j):
        kv_turned[j] = kv_ref[j].astype(F32).T.astype(BF16)
        dkv_ref[j] = jnp.zeros((k_tok, lanes), F32)

    @pl.loop(0, blocks)
    def _(i):
        start = i * (i + 1) // 2
        turned = qg_ref[i].astype(F32).T
        q_high = jnp.where(upper, turned * scale, 0.0)
        q_high_b = q_high.astype(BF16)

        def score(j, largest):
            block = dot(kv_ref[j], q_high_b)
            scores[j] = block
            return jnp.maximum(largest, jnp.max(block, axis=0, keepdims=True))

        largest = lax.fori_loop(0, i, score, jnp.full((1, q_tok), NEGATIVE, F32))
        last = jnp.where(visible, dot(kv_ref[i], q_high_b), NEGATIVE)
        scores[i] = last
        largest = jnp.maximum(largest, jnp.max(last, axis=0, keepdims=True))

        def weigh(j, carry):
            accum, length = carry
            block = jnp.exp(scores[j] - largest)
            length = length + jnp.sum(block, axis=0, keepdims=True)
            block = block.astype(BF16)
            weights[start + j] = block
            return accum + dot(kv_turned[j], block), length

        accum, length = lax.fori_loop(
            0, i + 1, weigh, (jnp.zeros((lanes, q_tok), F32), jnp.zeros((1, q_tok), F32))
        )
        inverse = 1.0 / length
        attended = (accum * inverse).astype(BF16).astype(F32)
        delta = jnp.sum(jnp.where(upper, 0.0, turned * attended), axis=0, keepdims=True) * inverse
        g_low = jnp.where(upper, 0.0, turned * inverse)
        g_low_b = g_low.astype(BF16)
        mixer = jnp.concatenate([q_high.T.astype(BF16), g_low.T.astype(BF16)], axis=0)

        def pull(j, accum):
            block = weights[start + j]
            grad = (block.astype(F32) * (dot(kv_ref[j], g_low_b) - delta)).astype(BF16)
            dkv_ref[j] += dot(jnp.concatenate([grad, block], axis=1), mixer)
            return accum + dot(kv_turned[j], grad)

        grad_q = lax.fori_loop(0, i + 1, pull, jnp.zeros((lanes, q_tok), F32))
        oq_ref[i] = jnp.where(upper, grad_q * scale, attended).T.astype(BF16)


def attention(qg, kv, frames, frame_part):
    blocks, q_tok, lanes = qg.shape
    k_tok = kv.shape[1]
    pairs = blocks * (blocks + 1) // 2
    return pl.pallas_call(
        functools.partial(attention_kernel, frames, frame_part, HEAD ** (-0.5)),
        out_shape=(
            jax.ShapeDtypeStruct((blocks, q_tok, lanes), BF16),
            jax.ShapeDtypeStruct((blocks, k_tok, lanes), F32),
        ),
        in_specs=[VMEM, VMEM],
        out_specs=(VMEM, VMEM),
        scratch_shapes=[
            pltpu.VMEM((pairs, k_tok, q_tok), BF16),
            pltpu.VMEM((blocks, k_tok, q_tok), F32),
            pltpu.VMEM((blocks, lanes, k_tok), BF16),
        ],
        compiler_params=pltpu.CompilerParams(vmem_limit_bytes=60 * 1024 * 1024),
        cost_estimate=pl.CostEstimate(
            flops=12 * pairs * k_tok * q_tok * lanes,
            bytes_accessed=4 * blocks * (q_tok + 2 * k_tok) * lanes,
            transcendentals=pairs * k_tok * q_tok,
        ),
    )(qg, kv)


def conv_kernel(adjoint, ext_ref, taps_ref, *rest):
    out_ref, total = rest[-2:]
    step = pl.program_id(0)
    _, frames, cols, rows, channels = ext_ref.shape
    frames, cols = frames - 2, cols - 2
    lag, row = step // 3, step % 3

    @pl.when(step == 0)
    def _():
        first = 0 if adjoint else 2
        centre = ext_ref[1, first : first + frames, 1 : 1 + cols]
        total[...] = centre.reshape(-1, channels).astype(F32)

    accum = total[...]
    for col in range(3):
        if adjoint:
            window = ext_ref[2 - row, pl.ds(2 - lag, frames), 2 - col : 2 - col + cols]
            sides = (((1,), (1,)), ((), ()))
        else:
            window = ext_ref[row, pl.ds(lag, frames), col : col + cols]
            sides = (((1,), (0,)), ((), ()))
        accum += lax.dot_general(
            window.reshape(-1, channels), taps_ref[0, col], sides, preferred_element_type=F32
        )
    total[...] = accum

    @pl.when(step == pl.num_programs(0) - 1)
    def _():
        result = total[...].astype(BF16)
        if adjoint:
            result = lax.dot_general(
                result, rest[0][...], (((1,), (1,)), ((), ())), preferred_element_type=F32
            ).astype(BF16)
        out_ref[...] = result


def convolve(extended, taps, out_proj=None):
    _, frames, cols, rows, channels = extended.shape
    tokens = (frames - 2) * (cols - 2) * rows
    adjoint = out_proj is not None
    width = out_proj.shape[0] if adjoint else channels
    whole = pl.BlockSpec(extended.shape, lambda g: (0, 0, 0, 0, 0))
    specs = [whole, pl.BlockSpec((1, 3, channels, channels), lambda g: (g, 0, 0, 0))]
    operands = [extended, taps.reshape(9, 3, channels, channels)]
    if adjoint:
        specs.append(pl.BlockSpec(out_proj.shape, lambda g: (0, 0)))
        operands.append(out_proj)
    return pl.pallas_call(
        functools.partial(conv_kernel, adjoint),
        grid=(9,),
        out_shape=jax.ShapeDtypeStruct((tokens, width), BF16),
        in_specs=specs,
        out_specs=pl.BlockSpec((tokens, width), lambda g: (0, 0)),
        scratch_shapes=[pltpu.VMEM((tokens, channels), F32)],
        compiler_params=pltpu.CompilerParams(vmem_limit_bytes=40 * 1024 * 1024),
        cost_estimate=pl.CostEstimate(
            flops=54 * tokens * channels * channels,
            bytes_accessed=54 * channels * channels,
            transcendentals=0,
        ),
    )(*operands)


def shifted(value, axis, steps, wrap):
    count = lax.axis_size(axis)
    pairs = [(i, (i + steps) % count) for i in range(count) if wrap or 0 <= i + steps < count]
    return lax.ppermute(value, axis, pairs)


def surrounded(field, adjoint):
    if adjoint:
        field = jnp.concatenate([field, shifted(field[:2], "tm", -1, False)], axis=0)
    else:
        field = jnp.concatenate([shifted(field[-2:], "tm", 1, False), field], axis=0)
    low = shifted(field[:, -1:], "space", 1, True)
    high = shifted(field[:, :1], "space", -1, True)
    field = jnp.concatenate([low, field, high], axis=1)
    zero = jnp.zeros_like(field[:, :, :1])
    above = jnp.concatenate([zero, field[:, :, :-1]], axis=2)
    below = jnp.concatenate([field[:, :, 1:], zero], axis=2)
    return jnp.stack([above, field, below])


def by_head(array, parts, spaces):
    frames, rows, cols, width = array.shape
    array = array.reshape(frames, parts, rows // parts, cols, -1, spaces, HEAD)
    array = array.transpose(4, 1, 5, 0, 2, 3, 6)
    return array.reshape(-1, frames * (rows // parts) * cols, HEAD)


def by_token(array, shape, parts, spaces):
    frames, rows, cols, width = shape
    array = array.reshape(-1, parts, spaces, frames, rows // parts, cols, HEAD)
    return array.transpose(3, 1, 4, 5, 0, 2, 6).reshape(shape)


def exchanged(array):
    return lax.all_to_all(array, ("tm", "space"), split_axis=0, concat_axis=0, tiled=True)


def to_sibling(array, parts, steps):
    count = lax.axis_size("tm")
    pairs = [(i, i // parts * parts + (i + steps) % parts) for i in range(count)]
    return lax.ppermute(array, "tm", pairs)


def shards(queries, key_rows, value_rows, out_proj, conv_taps, cotangent):
    frames, rows, cols, width = shape = queries.shape
    channels = out_proj.shape[1]
    cycle, spaces = lax.axis_size("tm"), lax.axis_size("space")
    parts = cycle * spaces // (width // HEAD)
    frame_part = rows // parts * cols

    turned = cotangent.transpose(0, 2, 1, 3)
    grad_attended = convolve(surrounded(turned, True), conv_taps, out_proj)
    grad_attended = grad_attended.reshape(frames, cols, rows, width).transpose(0, 2, 1, 3)

    packed = jnp.concatenate(
        [by_head(x, parts, spaces) for x in (queries, grad_attended, key_rows, value_rows)], axis=2
    )
    packed = exchanged(packed).reshape(cycle, -1, 4 * HEAD)
    kv = packed[:, :, 2 * HEAD :]
    kv = jnp.concatenate(
        [kv] + [to_sibling(kv, parts, -step) for step in range(1, parts)], axis=1
    )
    oq, dkv = attention(packed[:, :, : 2 * HEAD], kv, frames, frame_part)
    own = packed.shape[1]
    grad_kv = dkv[:, :own]
    for step in range(1, parts):
        piece = dkv[:, step * own : (step + 1) * own].astype(BF16)
        grad_kv = grad_kv + to_sibling(piece, parts, step).astype(F32)
    packed = jnp.concatenate([oq, grad_kv.astype(BF16)], axis=2)
    packed = exchanged(packed.reshape(cycle * spaces, -1, 4 * HEAD))
    grad_q, attended, grad_k, grad_v = (
        by_token(packed[:, :, i * HEAD : (i + 1) * HEAD], shape, parts, spaces) for i in range(4)
    )
    attended = attended.transpose(0, 2, 1, 3).reshape(-1, width)
    projected = dot(attended, out_proj).astype(BF16).reshape(frames, cols, rows, channels)
    conv_output = convolve(surrounded(projected, False), conv_taps)
    conv_output = conv_output.reshape(frames, cols, rows, channels).transpose(0, 2, 1, 3)
    return (conv_output, grad_q, grad_k, grad_v)


def solution(mesh):
    tokens = P("tm", None, "space", None)
    return jax.shard_map(
        shards,
        mesh=mesh,
        in_specs=(tokens, tokens, tokens, P(), P(), tokens),
        out_specs=(tokens, tokens, tokens, tokens),
        check_vma=False,
    )
```

```python
import functools

import jax
import jax.numpy as jnp
from jax import lax
from jax.experimental import pallas as pl
from jax.experimental.pallas import tpu as pltpu
from jax.sharding import PartitionSpec as P

HEAD = 64
NEGATIVE = -1e30
F32 = jnp.float32
BF16 = jnp.bfloat16
MESH = pl.DeviceIdType.MESH
VMEM = pl.BlockSpec(memory_space=pltpu.VMEM)


def dot(left, right):
    return jnp.dot(left, right, preferred_element_type=F32)


def everyone():
    cycle, spaces = lax.axis_size("tm"), lax.axis_size("space")
    me = lax.axis_index("tm") * spaces + lax.axis_index("space")
    return cycle * spaces, me


def place(index):
    spaces = lax.axis_size("space")
    return (index // spaces, lax.rem(index, spaces))


def greet_everyone():
    count, me = everyone()
    barrier = pltpu.get_barrier_semaphore()

    @pl.loop(1, count)
    def _(i):
        pl.semaphore_signal(
            barrier, inc=1, device_id=place(lax.rem(me + i, count)), device_id_type=MESH
        )

    pl.semaphore_wait(barrier, count - 1)


def remote(source, target, sems, where):
    return pltpu.make_async_remote_copy(
        src_ref=source,
        dst_ref=target,
        send_sem=sems[0],
        recv_sem=sems[1],
        device_id=where,
        device_id_type=MESH,
    )


def block_copy(send, recv, sems, i, arriving):
    count, me = everyone()
    other = lax.rem(me - i + count, count) if arriving else lax.rem(me + i, count)
    landing = other if arriving else me
    pair = (sems[0].at[i], sems[1].at[i])
    return remote(send.at[other], recv.at[landing], pair, place(other))


def start_exchange(send, recv, sems):
    count, me = everyone()

    @pl.loop(1, count)
    def _(i):
        block_copy(send, recv, sems, i, False).start()


def finish_exchange(send, recv, sems):
    count, me = everyone()

    @pl.loop(1, count)
    def _(i):
        block_copy(send, recv, sems, i, True).wait_recv()

    @pl.loop(1, count)
    def _(i):
        block_copy(send, recv, sems, i, False).wait_send()


def unfolded(block, fold):
    turned = block.reshape(-1, block.shape[-1]).astype(F32).T
    return jnp.concatenate([turned[k * HEAD : (k + 1) * HEAD] for k in range(fold)], axis=1)


def refolded(turned, fold, shape):
    width = turned.shape[1] // fold
    pieces = [turned[:, k * width : (k + 1) * width] for k in range(fold)]
    if fold == 1:
        pieces.append(jnp.zeros_like(pieces[0]))
    return jnp.concatenate(pieces, axis=0).T.astype(BF16).reshape(shape)


def attention_kernel(
    frames,
    frame_part,
    fold,
    scale,
    qkv_ref,
    g_ref,
    dq_ref,
    dkv_ref,
    o_recv,
    g_recv,
    o_send,
    keys,
    turned_keys,
    total,
    arrived,
    weights,
    maxima,
    lengths,
    attended,
    g_sems,
    o_sems,
    key_sems,
    part_sems,
):
    cycle, spaces = lax.axis_size("tm"), lax.axis_size("space")
    count, me = everyone()
    parts, _, n, lanes = keys.shape
    q_tok, k_tok = spaces * n, parts * spaces * n
    position, column = lax.axis_index("tm"), lax.axis_index("space")
    part = lax.rem(position, parts)

    def sibling(step):
        return (position - part + lax.rem(part + step + parts, parts), column)

    def key_copy(step):
        pair = (key_sems.at[0, step - 1], key_sems.at[1, step - 1])
        return remote(keys.at[0], keys.at[step], pair, sibling(step))

    def part_copy(step, j):
        pair = (part_sems.at[0, step - 1, j], part_sems.at[1, step - 1, j])
        rows = pl.ds(j * spaces, spaces)
        return remote(
            keys.at[step, rows], arrived.at[step - 1, rows], pair, sibling(-step)
        )

    def block_of(j):
        return pl.ds(j * spaces, spaces)

    def keys_of(j):
        return keys[:, block_of(j)].reshape(k_tok, lanes)

    @pl.loop(0, cycle)
    def _(j):
        keys[0, block_of(j)] = qkv_ref[block_of(j), :n]

    greet_everyone()
    for step in range(1, parts):
        key_copy(step).start()
    start_exchange(g_ref, g_recv, g_sems)
    g_recv[me] = g_ref[me]

    key_token = lax.broadcasted_iota(jnp.int32, (k_tok, q_tok), 0) % n
    query_token = lax.broadcasted_iota(jnp.int32, (k_tok, q_tok), 1)
    query_token = query_token // (q_tok // fold) * (n // fold) + query_token % (n // fold)
    visible = key_token // frame_part <= query_token // frame_part
    for step in range(1, parts):
        key_copy(step).wait()

    @pl.loop(0, cycle)
    def _(j):
        turned_keys[j] = keys_of(j).astype(F32).T.astype(BF16)
        total[j] = jnp.zeros((k_tok, lanes), F32)

    none = jnp.zeros((HEAD, q_tok), F32)

    def query_of(i):
        return jnp.concatenate([unfolded(qkv_ref[block_of(i), n:], fold) * scale, none], axis=0)

    @pl.loop(0, cycle)
    def _(i):
        start = i * (i + 1) // 2
        query = query_of(i).astype(BF16)

        def weigh(j, carry, scores):
            accum, length, largest = carry
            above = jnp.maximum(largest, jnp.max(scores, axis=0, keepdims=True))
            factor = jnp.exp(largest - above)
            block = jnp.exp(scores - above)
            length = length * factor + jnp.sum(block, axis=0, keepdims=True)
            block = block.astype(BF16)
            weights[start + j] = block
            maxima[start + j] = above
            return accum * factor + dot(turned_keys[j], block), length, above

        carry = (
            jnp.zeros((lanes, q_tok), F32),
            jnp.zeros((1, q_tok), F32),
            jnp.full((1, q_tok), NEGATIVE, F32),
        )
        carry = weigh(i, carry, jnp.where(visible, dot(keys_of(i), query), NEGATIVE))
        accum, length, largest = lax.fori_loop(
            0, i, lambda j, carry: weigh(j, carry, dot(keys_of(j), query)), carry
        )
        inverse = 1.0 / length
        result = accum[HEAD:] * inverse
        attended[i] = result.astype(BF16)
        lengths[0, i] = inverse
        lengths[1, i] = largest
        o_send[block_of(i)] = refolded(result, fold, (spaces, n // fold, lanes))

    o_recv[me] = o_send[me]
    start_exchange(o_send, o_recv, o_sems)
    finish_exchange(g_ref, g_recv, g_sems)

    @pl.loop(0, cycle)
    def _(back):
        i = cycle - 1 - back
        start = i * (i + 1) // 2
        query = query_of(i)
        grad_out = unfolded(g_recv[block_of(i)], fold)
        inverse, largest = lengths[0, i], lengths[1, i]
        delta = jnp.sum(grad_out * attended[i].astype(F32), axis=0, keepdims=True) * inverse
        grad_out = jnp.concatenate([none, grad_out * inverse], axis=0)
        grad_out_b = grad_out.astype(BF16)
        mixer = jnp.concatenate([query.T.astype(BF16), grad_out.T.astype(BF16)], axis=0)

        def pull(j, accum):
            factor = jnp.exp(maxima[start + j] - largest)
            block = weights[start + j].astype(F32) * factor
            grad = (block * (dot(keys_of(j), grad_out_b) - delta)).astype(BF16)
            total[j] += dot(jnp.concatenate([grad, block.astype(BF16)], axis=1), mixer)
            return accum + dot(turned_keys[j], grad)

        grad_q = lax.fori_loop(0, i + 1, pull, jnp.zeros((lanes, q_tok), F32))
        dq_ref[block_of(i)] = refolded(grad_q[:HEAD] * scale, fold, (spaces, n // fold, lanes))
        for step in range(1, parts):
            piece = total[i, step * q_tok : (step + 1) * q_tok]
            keys[step, block_of(i)] = piece.astype(BF16).reshape(spaces, n, lanes)
            part_copy(step, i).start()

    @pl.loop(0, cycle)
    def _(back):
        j = cycle - 1 - back
        summed = total[j, :q_tok]
        for step in range(1, parts):
            part_copy(step, j).wait()
            summed += arrived[step - 1, block_of(j)].reshape(q_tok, lanes).astype(F32)
        dkv_ref[block_of(j)] = summed.astype(BF16).reshape(spaces, n, lanes)

    finish_exchange(o_send, o_recv, o_sems)


def attention(qkv, g, frames, frame_part, fold, parts):
    cycle, spaces = lax.axis_size("tm"), lax.axis_size("space")
    count, some, lanes = g.shape
    n = some * fold
    q_tok, k_tok = spaces * n, parts * spaces * n
    pairs = cycle * (cycle + 1) // 2
    folded = (count, some, lanes)
    others = max(parts - 1, 1)
    return pl.pallas_call(
        functools.partial(attention_kernel, frames, frame_part, fold, HEAD ** (-0.5)),
        out_shape=(
            jax.ShapeDtypeStruct(folded, BF16),
            jax.ShapeDtypeStruct((count, n, lanes), BF16),
            jax.ShapeDtypeStruct(folded, BF16),
        ),
        in_specs=[VMEM, VMEM],
        out_specs=(VMEM, VMEM, VMEM),
        scratch_shapes=[
            pltpu.VMEM(folded, BF16),
            pltpu.VMEM(folded, BF16),
            pltpu.VMEM((parts, count, n, lanes), BF16),
            pltpu.VMEM((cycle, lanes, k_tok), BF16),
            pltpu.VMEM((cycle, k_tok, lanes), F32),
            pltpu.VMEM((others, count, n, lanes), BF16),
            pltpu.VMEM((pairs, k_tok, q_tok), BF16),
            pltpu.VMEM((pairs, 1, q_tok), F32),
            pltpu.VMEM((2, cycle, 1, q_tok), F32),
            pltpu.VMEM((cycle, HEAD, q_tok), BF16),
            [pltpu.SemaphoreType.DMA((count,))] * 2,
            [pltpu.SemaphoreType.DMA((count,))] * 2,
            pltpu.SemaphoreType.DMA((2, others)),
            pltpu.SemaphoreType.DMA((2, others, cycle)),
        ],
        compiler_params=pltpu.CompilerParams(
            vmem_limit_bytes=62 * 1024 * 1024, collective_id=1, has_side_effects=True
        ),
        cost_estimate=pl.CostEstimate(
            flops=12 * pairs * k_tok * q_tok * lanes,
            bytes_accessed=4 * count * n * lanes,
            transcendentals=pairs * k_tok * q_tok,
        ),
    )(qkv, g)


def conv_kernel(adjoint, field_ref, taps_ref, *rest):
    *mixing, send_ref, out_ref, recv_ref, around, shifted, total, near_sems, sems, own_sem = rest
    step = pl.program_id(0)
    frames, cols, rows, channels = field_ref.shape
    lag, row = step // 3, step % 3
    count, me = everyone()
    cycle, spaces = lax.axis_size("tm"), lax.axis_size("space")
    position, column = lax.axis_index("tm"), lax.axis_index("space")
    here, far, first = (0, frames, 0) if adjoint else (2, 0, frames - 2)
    ahead = lax.rem(position + (cycle - 1 if adjoint else 1), cycle)
    right, left = lax.rem(column + 1, spaces), lax.rem(column + spaces - 1, spaces)

    def halo():
        edge = pl.ds(first, 2)
        beyond = pl.ds(far, 2)
        within = pl.ds(here, frames)
        plan = (
            (field_ref.at[edge], around.at[beyond, pl.ds(1, cols)], (ahead, column)),
            (field_ref.at[:, cols - 1], around.at[within, 0], (position, right)),
            (field_ref.at[:, 0], around.at[within, cols + 1], (position, left)),
            (field_ref.at[edge, cols - 1], around.at[beyond, 0], (ahead, right)),
            (field_ref.at[edge, 0], around.at[beyond, cols + 1], (ahead, left)),
        )
        return [
            remote(source, target, (near_sems.at[0, k], near_sems.at[1, k]), where)
            for k, (source, target, where) in enumerate(plan)
        ]

    def own():
        return pltpu.make_async_copy(send_ref.at[me], recv_ref.at[me], own_sem)

    @pl.when(step == 0)
    def _():
        greet_everyone()
        for copy in halo():
            copy.start()
        own().start()
        start_exchange(send_ref, recv_ref, sems)
        centre = field_ref[...]
        around[here : here + frames, 1 : 1 + cols] = centre
        total[...] = centre.reshape(-1, channels).astype(F32)
        for copy in halo():
            copy.wait()
        outside = position == (cycle - 1 if adjoint else 0)
        beyond = around[far : far + 2]
        around[far : far + 2] = jnp.where(outside, jnp.zeros_like(beyond), beyond)
        for frame in range(frames + 2):
            whole = around[frame]
            flat = whole.astype(F32).reshape(-1, channels)
            place_in = lax.broadcasted_iota(jnp.int32, flat.shape, 0) % rows
            above = jnp.where(place_in == 0, 0.0, pltpu.roll(flat, 1, 0))
            below = jnp.where(place_in == rows - 1, 0.0, pltpu.roll(flat, flat.shape[0] - 1, 0))
            shifted[0, frame] = above.astype(BF16).reshape(whole.shape)
            shifted[1, frame] = whole
            shifted[2, frame] = below.astype(BF16).reshape(whole.shape)

    accum = total[...]
    for col in range(3):
        if adjoint:
            window = shifted[2 - row, pl.ds(2 - lag, frames), 2 - col : 2 - col + cols]
            sides = (((1,), (1,)), ((), ()))
        else:
            window = shifted[row, pl.ds(lag, frames), col : col + cols]
            sides = (((1,), (0,)), ((), ()))
        accum += lax.dot_general(
            window.reshape(-1, channels), taps_ref[0, col], sides, preferred_element_type=F32
        )
    total[...] = accum

    @pl.when(step == pl.num_programs(0) - 1)
    def _():
        result = total[...].astype(BF16)
        if adjoint:
            result = lax.dot_general(
                result, mixing[0][...], (((1,), (1,)), ((), ())), preferred_element_type=F32
            ).astype(BF16)
        out_ref[...] = result
        own().wait()
        finish_exchange(send_ref, recv_ref, sems)


def convolve(field, taps, send, out_proj=None):
    frames, cols, rows, channels = field.shape
    tokens = frames * cols * rows
    count = send.shape[0]
    adjoint = out_proj is not None
    width = out_proj.shape[0] if adjoint else channels
    specs = [
        pl.BlockSpec(field.shape, lambda g: (0, 0, 0, 0)),
        pl.BlockSpec((1, 3, channels, channels), lambda g: (g, 0, 0, 0)),
    ]
    operands = [field, taps.reshape(9, 3, channels, channels)]
    if adjoint:
        specs.append(pl.BlockSpec(out_proj.shape, lambda g: (0, 0)))
        operands.append(out_proj)
    around = (frames + 2, cols + 2, rows, channels)
    return pl.pallas_call(
        functools.partial(conv_kernel, adjoint),
        grid=(9,),
        out_shape=(
            jax.ShapeDtypeStruct((tokens, width), BF16),
            jax.ShapeDtypeStruct(send.shape, BF16),
        ),
        in_specs=specs + [pl.BlockSpec(memory_space=pl.ANY)],
        out_specs=(
            pl.BlockSpec((tokens, width), lambda g: (0, 0)),
            pl.BlockSpec(memory_space=pl.ANY),
        ),
        scratch_shapes=[
            pltpu.VMEM(around, BF16),
            pltpu.VMEM((3,) + around, BF16),
            pltpu.VMEM((tokens, channels), F32),
            pltpu.SemaphoreType.DMA((2, 5)),
            [pltpu.SemaphoreType.DMA((count,))] * 2,
            pltpu.SemaphoreType.DMA,
        ],
        compiler_params=pltpu.CompilerParams(
            vmem_limit_bytes=40 * 1024 * 1024,
            collective_id=0 if adjoint else 2,
            has_side_effects=True,
        ),
        cost_estimate=pl.CostEstimate(
            flops=54 * tokens * channels * channels,
            bytes_accessed=54 * channels * channels,
            transcendentals=0,
        ),
    )(*operands, send)


def by_head(array, parts, spaces):
    frames, rows, cols, width = array.shape
    array = array.reshape(frames, parts, rows // parts, cols, -1, spaces, HEAD)
    array = array.transpose(4, 1, 5, 0, 2, 3, 6)
    return array.reshape(-1, frames * (rows // parts) * cols, HEAD)


def by_token(array, shape, parts, spaces):
    frames, rows, cols, width = shape
    array = array.reshape(-1, parts, spaces, frames, rows // parts, cols, HEAD)
    return array.transpose(3, 1, 4, 5, 0, 2, 6).reshape(shape)


def folded(array, fold):
    size = array.shape[1] // fold
    pieces = [array[:, k * size : (k + 1) * size] for k in range(fold)]
    if fold == 1:
        pieces.append(jnp.zeros_like(array))
    return jnp.concatenate(pieces, axis=2)


def opened(array, fold):
    return jnp.concatenate([array[:, :, k * HEAD : (k + 1) * HEAD] for k in range(fold)], axis=1)


def shards(queries, key_rows, value_rows, out_proj, conv_taps, cotangent):
    frames, rows, cols, width = shape = queries.shape
    channels = out_proj.shape[1]
    cycle, spaces = lax.axis_size("tm"), lax.axis_size("space")
    parts = cycle * spaces // (width // HEAD)
    frame_part = rows // parts * cols
    n = frames * frame_part
    fold = 2 if n % 32 == 0 else 1

    q, k, v = (by_head(x, parts, spaces) for x in (queries, key_rows, value_rows))
    qkv = jnp.concatenate([jnp.concatenate([k, v], axis=2), folded(q, fold)], axis=1)
    grad_attended, qkv = convolve(cotangent.transpose(0, 2, 1, 3), conv_taps, qkv, out_proj)
    grad_attended = grad_attended.reshape(frames, cols, rows, width).transpose(0, 2, 1, 3)
    g = folded(by_head(grad_attended, parts, spaces), fold)
    dq, dkv, attended = attention(qkv, g, frames, frame_part, fold, parts)

    attended = by_token(opened(attended, fold), shape, parts, spaces)
    attended = attended.transpose(0, 2, 1, 3).reshape(-1, width)
    projected = dot(attended, out_proj).astype(BF16).reshape(frames, cols, rows, channels)
    conv_output, grads = convolve(projected, conv_taps, jnp.concatenate([dkv, dq], axis=1))
    conv_output = conv_output.reshape(frames, cols, rows, channels).transpose(0, 2, 1, 3)
    grad_k, grad_v, grad_q = (
        by_token(x, shape, parts, spaces)
        for x in (grads[:, :n, :HEAD], grads[:, :n, HEAD:], opened(grads[:, n:], fold))
    )
    return (conv_output, grad_q, grad_k, grad_v)


def solution(mesh):
    tokens = P("tm", None, "space", None)
    return jax.shard_map(
        shards,
        mesh=mesh,
        in_specs=(tokens, tokens, tokens, P(), P(), tokens),
        out_specs=(tokens, tokens, tokens, tokens),
        check_vma=False,
    )
```

```python
import functools

import jax
import jax.numpy as jnp
from jax import lax
from jax.experimental import pallas as pl
from jax.experimental.pallas import tpu as pltpu
from jax.sharding import PartitionSpec as P

HEAD = 64
NEGATIVE = -1e30
F32 = jnp.float32
BF16 = jnp.bfloat16
MESH = pl.DeviceIdType.MESH
VMEM = pl.BlockSpec(memory_space=pltpu.VMEM)


def dot(left, right):
    return jnp.dot(left, right, preferred_element_type=F32)


def everyone():
    cycle, spaces = lax.axis_size("tm"), lax.axis_size("space")
    me = lax.axis_index("tm") * spaces + lax.axis_index("space")
    return cycle * spaces, me


def place(index):
    spaces = lax.axis_size("space")
    return (index // spaces, lax.rem(index, spaces))


def greet_everyone():
    count, me = everyone()
    barrier = pltpu.get_barrier_semaphore()

    @pl.loop(1, count)
    def _(i):
        pl.semaphore_signal(
            barrier, inc=1, device_id=place(lax.rem(me + i, count)), device_id_type=MESH
        )

    pl.semaphore_wait(barrier, count - 1)


def remote(source, target, sems, where):
    return pltpu.make_async_remote_copy(
        src_ref=source,
        dst_ref=target,
        send_sem=sems[0],
        recv_sem=sems[1],
        device_id=where,
        device_id_type=MESH,
    )


def block_copy(send, recv, sems, i, arriving):
    count, me = everyone()
    other = lax.rem(me - i + count, count) if arriving else lax.rem(me + i, count)
    landing = other if arriving else me
    pair = (sems[0].at[i], sems[1].at[i])
    return remote(send.at[other], recv.at[landing], pair, place(other))


def start_exchange(send, recv, sems):
    count, me = everyone()

    @pl.loop(1, count)
    def _(i):
        block_copy(send, recv, sems, i, False).start()


def finish_exchange(send, recv, sems):
    count, me = everyone()

    @pl.loop(1, count)
    def _(i):
        block_copy(send, recv, sems, i, True).wait_recv()

    @pl.loop(1, count)
    def _(i):
        block_copy(send, recv, sems, i, False).wait_send()


def unfolded(block, fold):
    turned = block.reshape(-1, block.shape[-1]).astype(F32).T
    return jnp.concatenate([turned[k * HEAD : (k + 1) * HEAD] for k in range(fold)], axis=1)


def refolded(turned, fold, shape):
    width = turned.shape[1] // fold
    pieces = [turned[:, k * width : (k + 1) * width] for k in range(fold)]
    if fold == 1:
        pieces.append(jnp.zeros_like(pieces[0]))
    return jnp.concatenate(pieces, axis=0).T.astype(BF16).reshape(shape)


def attention_kernel(
    frames,
    frame_part,
    fold,
    scale,
    qkv_ref,
    g_ref,
    dq_ref,
    dkv_ref,
    o_recv,
    g_recv,
    o_send,
    keys,
    turned_keys,
    total,
    arrived,
    weights,
    maxima,
    lengths,
    attended,
    g_sems,
    o_sems,
    key_sems,
    part_sems,
):
    cycle, spaces = lax.axis_size("tm"), lax.axis_size("space")
    count, me = everyone()
    parts, _, n, lanes = keys.shape
    q_tok, k_tok = spaces * n, parts * spaces * n
    position, column = lax.axis_index("tm"), lax.axis_index("space")
    part = lax.rem(position, parts)
    group = 4 if cycle % 4 == 0 and cycle < 16 else 2 if cycle % 2 == 0 else 1

    def sibling(step):
        return (position - part + lax.rem(part + step + parts, parts), column)

    def key_copy(step):
        pair = (key_sems.at[0, step - 1], key_sems.at[1, step - 1])
        return remote(keys.at[0], keys.at[step], pair, sibling(step))

    def part_copy(step, j):
        pair = (part_sems.at[0, step - 1, j], part_sems.at[1, step - 1, j])
        rows = pl.ds(j * spaces, spaces)
        return remote(
            keys.at[step, rows], arrived.at[step - 1, rows], pair, sibling(-step)
        )

    def block_of(j):
        return pl.ds(j * spaces, spaces)

    def keys_of(j):
        return keys[:, block_of(j)].reshape(k_tok, lanes)

    @pl.loop(0, cycle)
    def _(j):
        keys[0, block_of(j)] = qkv_ref[block_of(j), :n]

    greet_everyone()
    for step in range(1, parts):
        key_copy(step).start()
    start_exchange(g_ref, g_recv, g_sems)
    g_recv[me] = g_ref[me]

    key_token = lax.broadcasted_iota(jnp.int32, (k_tok, q_tok), 0) % n
    query_token = lax.broadcasted_iota(jnp.int32, (k_tok, q_tok), 1)
    query_token = query_token // (q_tok // fold) * (n // fold) + query_token % (n // fold)
    visible = key_token // frame_part <= query_token // frame_part
    for step in range(1, parts):
        key_copy(step).wait()

    @pl.loop(0, cycle)
    def _(j):
        turned_keys[j] = keys_of(j).astype(F32).T.astype(BF16)
        total[j] = jnp.zeros((k_tok, lanes), F32)

    none = jnp.zeros((HEAD, q_tok), F32)

    def query_of(i):
        return jnp.concatenate([unfolded(qkv_ref[block_of(i), n:], fold) * scale, none], axis=0)

    def slot(i, j):
        return i * (i + 1) // 2 + j

    @pl.loop(0, cycle // group)
    def _(several):
        base = several * group
        queries = [query_of(base + m).astype(BF16) for m in range(group)]

        def weigh(j, carry, members, masked=None):
            carry = list(carry)
            key_block, turned_block = keys_of(j), turned_keys[j]
            for m in members:
                accum, length, largest = carry[m]
                scores = dot(key_block, queries[m])
                if m == masked:
                    scores = jnp.where(visible, scores, NEGATIVE)
                above = jnp.maximum(largest, jnp.max(scores, axis=0, keepdims=True))
                factor = jnp.exp(largest - above)
                block = jnp.exp(scores - above)
                length = length * factor + jnp.sum(block, axis=0, keepdims=True)
                block = block.astype(BF16)
                weights[slot(base + m, j)] = block
                maxima[slot(base + m, j)] = above
                carry[m] = (accum * factor + dot(turned_block, block), length, above)
            return tuple(carry)

        carry = (
            (
                jnp.zeros((lanes, q_tok), F32),
                jnp.zeros((1, q_tok), F32),
                jnp.full((1, q_tok), NEGATIVE, F32),
            ),
        ) * group
        for m in range(group):
            carry = weigh(base + m, carry, range(m, group), m)
        carry = lax.fori_loop(0, base, lambda j, carry: weigh(j, carry, range(group)), carry)
        for m, (accum, length, largest) in enumerate(carry):
            i = base + m
            inverse = 1.0 / length
            result = accum[HEAD:] * inverse
            attended[i] = result.astype(BF16)
            lengths[0, i] = inverse
            lengths[1, i] = largest
            o_send[block_of(i)] = refolded(result, fold, (spaces, n // fold, lanes))

    o_recv[me] = o_send[me]
    start_exchange(o_send, o_recv, o_sems)
    finish_exchange(g_ref, g_recv, g_sems)

    @pl.loop(0, cycle // group)
    def _(back):
        base = (cycle // group - 1 - back) * group
        grads, mixers, deltas, limits = [], [], [], []
        for m in range(group):
            i = base + m
            query = query_of(i)
            grad_out = unfolded(g_recv[block_of(i)], fold)
            inverse = lengths[0, i]
            delta = jnp.sum(grad_out * attended[i].astype(F32), axis=0, keepdims=True) * inverse
            grad_out = jnp.concatenate([none, grad_out * inverse], axis=0)
            grads.append(grad_out.astype(BF16))
            mixers += [query.T.astype(BF16), grad_out.T.astype(BF16)]
            deltas.append(delta)
            limits.append(lengths[1, i])
        mixer = jnp.concatenate(mixers, axis=0)

        def pull(j, carry, members):
            carry = list(carry)
            key_block, turned_block = keys_of(j), turned_keys[j]
            mixed = []
            for m in members:
                factor = jnp.exp(maxima[slot(base + m, j)] - limits[m])
                block = weights[slot(base + m, j)].astype(F32) * factor
                grad = (block * (dot(key_block, grads[m]) - deltas[m])).astype(BF16)
                mixed += [grad, block.astype(BF16)]
                carry[m] = carry[m] + dot(turned_block, grad)
            total[j] += dot(jnp.concatenate(mixed, axis=1), mixer[2 * members[0] * q_tok :])
            return tuple(carry)

        carry = (jnp.zeros((lanes, q_tok), F32),) * group
        carry = lax.fori_loop(0, base, lambda j, carry: pull(j, carry, range(group)), carry)
        for m in range(group):
            carry = pull(base + m, carry, range(m, group))
        for m in range(group):
            i = base + m
            dq_ref[block_of(i)] = refolded(
                carry[m][:HEAD] * scale, fold, (spaces, n // fold, lanes)
            )
            for step in range(1, parts):
                piece = total[i, step * q_tok : (step + 1) * q_tok]
                keys[step, block_of(i)] = piece.astype(BF16).reshape(spaces, n, lanes)
                part_copy(step, i).start()

    @pl.loop(0, cycle)
    def _(back):
        j = cycle - 1 - back
        summed = total[j, :q_tok]
        for step in range(1, parts):
            part_copy(step, j).wait()
            summed += arrived[step - 1, block_of(j)].reshape(q_tok, lanes).astype(F32)
        dkv_ref[block_of(j)] = summed.astype(BF16).reshape(spaces, n, lanes)

    finish_exchange(o_send, o_recv, o_sems)


def attention(qkv, g, frames, frame_part, fold, parts):
    cycle, spaces = lax.axis_size("tm"), lax.axis_size("space")
    count, some, lanes = g.shape
    n = some * fold
    q_tok, k_tok = spaces * n, parts * spaces * n
    pairs = cycle * (cycle + 1) // 2
    folded = (count, some, lanes)
    others = max(parts - 1, 1)
    return pl.pallas_call(
        functools.partial(attention_kernel, frames, frame_part, fold, HEAD ** (-0.5)),
        out_shape=(
            jax.ShapeDtypeStruct(folded, BF16),
            jax.ShapeDtypeStruct((count, n, lanes), BF16),
            jax.ShapeDtypeStruct(folded, BF16),
        ),
        in_specs=[VMEM, VMEM],
        out_specs=(VMEM, VMEM, VMEM),
        scratch_shapes=[
            pltpu.VMEM(folded, BF16),
            pltpu.VMEM(folded, BF16),
            pltpu.VMEM((parts, count, n, lanes), BF16),
            pltpu.VMEM((cycle, lanes, k_tok), BF16),
            pltpu.VMEM((cycle, k_tok, lanes), F32),
            pltpu.VMEM((others, count, n, lanes), BF16),
            pltpu.VMEM((pairs, k_tok, q_tok), BF16),
            pltpu.VMEM((pairs, 1, q_tok), F32),
            pltpu.VMEM((2, cycle, 1, q_tok), F32),
            pltpu.VMEM((cycle, HEAD, q_tok), BF16),
            [pltpu.SemaphoreType.DMA((count,))] * 2,
            [pltpu.SemaphoreType.DMA((count,))] * 2,
            pltpu.SemaphoreType.DMA((2, others)),
            pltpu.SemaphoreType.DMA((2, others, cycle)),
        ],
        compiler_params=pltpu.CompilerParams(
            vmem_limit_bytes=62 * 1024 * 1024, collective_id=1, has_side_effects=True
        ),
        cost_estimate=pl.CostEstimate(
            flops=12 * pairs * k_tok * q_tok * lanes,
            bytes_accessed=4 * count * n * lanes,
            transcendentals=pairs * k_tok * q_tok,
        ),
    )(qkv, g)


def conv_kernel(adjoint, field_ref, taps_ref, *rest):
    *mixing, send_ref, out_ref, recv_ref, around, shifted, total, near_sems, sems, own_sem = rest
    step = pl.program_id(0)
    frames, cols, rows, channels = field_ref.shape
    lag, row = step // 3, step % 3
    count, me = everyone()
    cycle, spaces = lax.axis_size("tm"), lax.axis_size("space")
    position, column = lax.axis_index("tm"), lax.axis_index("space")
    here, far, first = (0, frames, 0) if adjoint else (2, 0, frames - 2)
    ahead = lax.rem(position + (cycle - 1 if adjoint else 1), cycle)
    right, left = lax.rem(column + 1, spaces), lax.rem(column + spaces - 1, spaces)

    def halo():
        edge = pl.ds(first, 2)
        beyond = pl.ds(far, 2)
        within = pl.ds(here, frames)
        plan = (
            (field_ref.at[edge], around.at[beyond, pl.ds(1, cols)], (ahead, column)),
            (field_ref.at[:, cols - 1], around.at[within, 0], (position, right)),
            (field_ref.at[:, 0], around.at[within, cols + 1], (position, left)),
            (field_ref.at[edge, cols - 1], around.at[beyond, 0], (ahead, right)),
            (field_ref.at[edge, 0], around.at[beyond, cols + 1], (ahead, left)),
        )
        return [
            remote(source, target, (near_sems.at[0, k], near_sems.at[1, k]), where)
            for k, (source, target, where) in enumerate(plan)
        ]

    def own():
        return pltpu.make_async_copy(send_ref.at[me], recv_ref.at[me], own_sem)

    @pl.when(step == 0)
    def _():
        greet_everyone()
        for copy in halo():
            copy.start()
        own().start()
        start_exchange(send_ref, recv_ref, sems)
        centre = field_ref[...]
        around[here : here + frames, 1 : 1 + cols] = centre
        total[...] = centre.reshape(-1, channels).astype(F32)
        for copy in halo():
            copy.wait()
        outside = position == (cycle - 1 if adjoint else 0)
        beyond = around[far : far + 2]
        around[far : far + 2] = jnp.where(outside, jnp.zeros_like(beyond), beyond)
        for frame in range(frames + 2):
            whole = around[frame]
            flat = whole.astype(F32).reshape(-1, channels)
            place_in = lax.broadcasted_iota(jnp.int32, flat.shape, 0) % rows
            above = jnp.where(place_in == 0, 0.0, pltpu.roll(flat, 1, 0))
            below = jnp.where(place_in == rows - 1, 0.0, pltpu.roll(flat, flat.shape[0] - 1, 0))
            shifted[0, frame] = above.astype(BF16).reshape(whole.shape)
            shifted[1, frame] = whole
            shifted[2, frame] = below.astype(BF16).reshape(whole.shape)

    accum = total[...]
    for col in range(3):
        if adjoint:
            window = shifted[2 - row, pl.ds(2 - lag, frames), 2 - col : 2 - col + cols]
            sides = (((1,), (1,)), ((), ()))
        else:
            window = shifted[row, pl.ds(lag, frames), col : col + cols]
            sides = (((1,), (0,)), ((), ()))
        accum += lax.dot_general(
            window.reshape(-1, channels), taps_ref[0, col], sides, preferred_element_type=F32
        )
    total[...] = accum

    @pl.when(step == pl.num_programs(0) - 1)
    def _():
        result = total[...].astype(BF16)
        if adjoint:
            result = lax.dot_general(
                result, mixing[0][...], (((1,), (1,)), ((), ())), preferred_element_type=F32
            ).astype(BF16)
        out_ref[...] = result
        own().wait()
        finish_exchange(send_ref, recv_ref, sems)


def convolve(field, taps, send, out_proj=None):
    frames, cols, rows, channels = field.shape
    tokens = frames * cols * rows
    count = send.shape[0]
    adjoint = out_proj is not None
    width = out_proj.shape[0] if adjoint else channels
    specs = [
        pl.BlockSpec(field.shape, lambda g: (0, 0, 0, 0)),
        pl.BlockSpec((1, 3, channels, channels), lambda g: (g, 0, 0, 0)),
    ]
    operands = [field, taps.reshape(9, 3, channels, channels)]
    if adjoint:
        specs.append(pl.BlockSpec(out_proj.shape, lambda g: (0, 0)))
        operands.append(out_proj)
    around = (frames + 2, cols + 2, rows, channels)
    return pl.pallas_call(
        functools.partial(conv_kernel, adjoint),
        grid=(9,),
        out_shape=(
            jax.ShapeDtypeStruct((tokens, width), BF16),
            jax.ShapeDtypeStruct(send.shape, BF16),
        ),
        in_specs=specs + [pl.BlockSpec(memory_space=pl.ANY)],
        out_specs=(
            pl.BlockSpec((tokens, width), lambda g: (0, 0)),
            pl.BlockSpec(memory_space=pl.ANY),
        ),
        scratch_shapes=[
            pltpu.VMEM(around, BF16),
            pltpu.VMEM((3,) + around, BF16),
            pltpu.VMEM((tokens, channels), F32),
            pltpu.SemaphoreType.DMA((2, 5)),
            [pltpu.SemaphoreType.DMA((count,))] * 2,
            pltpu.SemaphoreType.DMA,
        ],
        compiler_params=pltpu.CompilerParams(
            vmem_limit_bytes=40 * 1024 * 1024,
            collective_id=0 if adjoint else 2,
            has_side_effects=True,
        ),
        cost_estimate=pl.CostEstimate(
            flops=54 * tokens * channels * channels,
            bytes_accessed=54 * channels * channels,
            transcendentals=0,
        ),
    )(*operands, send)


def by_head(array, parts, spaces):
    frames, rows, cols, width = array.shape
    array = array.reshape(frames, parts, rows // parts, cols, -1, spaces, HEAD)
    array = array.transpose(4, 1, 5, 0, 2, 3, 6)
    return array.reshape(-1, frames * (rows // parts) * cols, HEAD)


def by_token(array, shape, parts, spaces):
    frames, rows, cols, width = shape
    array = array.reshape(-1, parts, spaces, frames, rows // parts, cols, HEAD)
    return array.transpose(3, 1, 4, 5, 0, 2, 6).reshape(shape)


def folded(array, fold):
    size = array.shape[1] // fold
    pieces = [array[:, k * size : (k + 1) * size] for k in range(fold)]
    if fold == 1:
        pieces.append(jnp.zeros_like(array))
    return jnp.concatenate(pieces, axis=2)


def opened(array, fold):
    return jnp.concatenate([array[:, :, k * HEAD : (k + 1) * HEAD] for k in range(fold)], axis=1)


def shards(queries, key_rows, value_rows, out_proj, conv_taps, cotangent):
    frames, rows, cols, width = shape = queries.shape
    channels = out_proj.shape[1]
    cycle, spaces = lax.axis_size("tm"), lax.axis_size("space")
    parts = cycle * spaces // (width // HEAD)
    frame_part = rows // parts * cols
    n = frames * frame_part
    fold = 2 if n % 32 == 0 else 1

    q, k, v = (by_head(x, parts, spaces) for x in (queries, key_rows, value_rows))
    qkv = jnp.concatenate([jnp.concatenate([k, v], axis=2), folded(q, fold)], axis=1)
    grad_attended, qkv = convolve(cotangent.transpose(0, 2, 1, 3), conv_taps, qkv, out_proj)
    grad_attended = grad_attended.reshape(frames, cols, rows, width).transpose(0, 2, 1, 3)
    g = folded(by_head(grad_attended, parts, spaces), fold)
    dq, dkv, attended = attention(qkv, g, frames, frame_part, fold, parts)

    attended = by_token(opened(attended, fold), shape, parts, spaces)
    attended = attended.transpose(0, 2, 1, 3).reshape(-1, width)
    projected = dot(attended, out_proj).astype(BF16).reshape(frames, cols, rows, channels)
    conv_output, grads = convolve(projected, conv_taps, jnp.concatenate([dkv, dq], axis=1))
    conv_output = conv_output.reshape(frames, cols, rows, channels).transpose(0, 2, 1, 3)
    grad_k, grad_v, grad_q = (
        by_token(x, shape, parts, spaces)
        for x in (grads[:, :n, :HEAD], grads[:, :n, HEAD:], opened(grads[:, n:], fold))
    )
    return (conv_output, grad_q, grad_k, grad_v)


def solution(mesh):
    tokens = P("tm", None, "space", None)
    return jax.shard_map(
        shards,
        mesh=mesh,
        in_specs=(tokens, tokens, tokens, P(), P(), tokens),
        out_specs=(tokens, tokens, tokens, tokens),
        check_vma=False,
    )
```

```python
import functools

import jax
import jax.numpy as jnp
from jax import lax
from jax.experimental import pallas as pl
from jax.experimental.pallas import tpu as pltpu
from jax.sharding import PartitionSpec as P

HEAD = 64
NEGATIVE = -1e30
F32 = jnp.float32
BF16 = jnp.bfloat16
MESH = pl.DeviceIdType.MESH
VMEM = pl.BlockSpec(memory_space=pltpu.VMEM)


def dot(left, right):
    return jnp.dot(left, right, preferred_element_type=F32)


def everyone():
    cycle, spaces = lax.axis_size("tm"), lax.axis_size("space")
    me = lax.axis_index("tm") * spaces + lax.axis_index("space")
    return cycle * spaces, me


def place(index):
    spaces = lax.axis_size("space")
    return (index // spaces, lax.rem(index, spaces))


def greet_everyone():
    count, me = everyone()
    barrier = pltpu.get_barrier_semaphore()

    @pl.loop(1, count)
    def _(i):
        pl.semaphore_signal(
            barrier, inc=1, device_id=place(lax.rem(me + i, count)), device_id_type=MESH
        )

    pl.semaphore_wait(barrier, count - 1)


def remote(source, target, sems, where):
    return pltpu.make_async_remote_copy(
        src_ref=source,
        dst_ref=target,
        send_sem=sems[0],
        recv_sem=sems[1],
        device_id=where,
        device_id_type=MESH,
    )


def block_copy(send, recv, sems, i, arriving):
    count, me = everyone()
    other = lax.rem(me - i + count, count) if arriving else lax.rem(me + i, count)
    landing = other if arriving else me
    pair = (sems[0].at[i], sems[1].at[i])
    return remote(send.at[other], recv.at[landing], pair, place(other))


def start_exchange(send, recv, sems):
    count, me = everyone()

    @pl.loop(1, count)
    def _(i):
        block_copy(send, recv, sems, i, False).start()


def finish_exchange(send, recv, sems):
    count, me = everyone()

    @pl.loop(1, count)
    def _(i):
        block_copy(send, recv, sems, i, True).wait_recv()

    @pl.loop(1, count)
    def _(i):
        block_copy(send, recv, sems, i, False).wait_send()


def unfolded(block, fold):
    turned = block.reshape(-1, block.shape[-1]).astype(F32).T
    return jnp.concatenate([turned[k * HEAD : (k + 1) * HEAD] for k in range(fold)], axis=1)


def refolded(turned, fold, shape):
    width = turned.shape[1] // fold
    pieces = [turned[:, k * width : (k + 1) * width] for k in range(fold)]
    if fold == 1:
        pieces.append(jnp.zeros_like(pieces[0]))
    return jnp.concatenate(pieces, axis=0).T.astype(BF16).reshape(shape)


def attention_kernel(
    frames,
    frame_part,
    fold,
    scale,
    qkv_ref,
    g_ref,
    dq_ref,
    dkv_ref,
    o_recv,
    g_recv,
    o_send,
    keys,
    turned_keys,
    total,
    arrived,
    weights,
    maxima,
    lengths,
    attended,
    g_sems,
    o_sems,
    key_sems,
    part_sems,
):
    cycle, spaces = lax.axis_size("tm"), lax.axis_size("space")
    count, me = everyone()
    parts, _, n, lanes = keys.shape
    q_tok, k_tok = spaces * n, parts * spaces * n
    position, column = lax.axis_index("tm"), lax.axis_index("space")
    part = lax.rem(position, parts)
    group = 4 if cycle % 4 == 0 and cycle < 16 else 2 if cycle % 2 == 0 else 1

    def sibling(step):
        return (position - part + lax.rem(part + step + parts, parts), column)

    def key_copy(step):
        pair = (key_sems.at[0, step - 1], key_sems.at[1, step - 1])
        return remote(keys.at[0], keys.at[step], pair, sibling(step))

    def part_copy(step, j):
        pair = (part_sems.at[0, step - 1, j], part_sems.at[1, step - 1, j])
        rows = pl.ds(j * spaces, spaces)
        return remote(
            keys.at[step, rows], arrived.at[step - 1, rows], pair, sibling(-step)
        )

    def block_of(j):
        return pl.ds(j * spaces, spaces)

    def keys_of(j):
        return keys[:, block_of(j)].reshape(k_tok, lanes)

    @pl.loop(0, cycle)
    def _(j):
        keys[0, block_of(j)] = qkv_ref[block_of(j), :n]

    greet_everyone()
    for step in range(1, parts):
        key_copy(step).start()
    start_exchange(g_ref, g_recv, g_sems)
    g_recv[me] = g_ref[me]

    key_token = lax.broadcasted_iota(jnp.int32, (k_tok, q_tok), 0) % n
    query_token = lax.broadcasted_iota(jnp.int32, (k_tok, q_tok), 1)
    query_token = query_token // (q_tok // fold) * (n // fold) + query_token % (n // fold)
    visible = key_token // frame_part <= query_token // frame_part
    for step in range(1, parts):
        key_copy(step).wait()

    @pl.loop(0, cycle)
    def _(j):
        turned_keys[j] = keys_of(j).astype(F32).T.astype(BF16)
        total[j] = jnp.zeros((k_tok, lanes), F32)

    none = jnp.zeros((HEAD, q_tok), F32)

    def query_of(i):
        return jnp.concatenate([unfolded(qkv_ref[block_of(i), n:], fold) * scale, none], axis=0)

    def slot(i, j):
        return i * (i + 1) // 2 + j

    @pl.loop(0, cycle // group)
    def _(several):
        base = several * group
        queries = [query_of(base + m).astype(BF16) for m in range(group)]

        def weigh(j, carry, members, masked=None):
            carry = list(carry)
            key_block, turned_block = keys_of(j), turned_keys[j]
            for m in members:
                accum, length, largest = carry[m]
                scores = dot(key_block, queries[m])
                if m == masked:
                    scores = jnp.where(visible, scores, NEGATIVE)
                above = jnp.maximum(largest, jnp.max(scores, axis=0, keepdims=True))
                factor = jnp.exp(largest - above)
                block = jnp.exp(scores - above)
                length = length * factor + jnp.sum(block, axis=0, keepdims=True)
                block = block.astype(BF16)
                weights[slot(base + m, j)] = block
                maxima[slot(base + m, j)] = above
                carry[m] = (accum * factor + dot(turned_block, block), length, above)
            return tuple(carry)

        carry = (
            (
                jnp.zeros((lanes, q_tok), F32),
                jnp.zeros((1, q_tok), F32),
                jnp.full((1, q_tok), NEGATIVE, F32),
            ),
        ) * group
        for m in range(group):
            carry = weigh(base + m, carry, range(m, group), m)
        carry = lax.fori_loop(0, base, lambda j, carry: weigh(j, carry, range(group)), carry)
        for m, (accum, length, largest) in enumerate(carry):
            i = base + m
            inverse = 1.0 / length
            result = accum[HEAD:] * inverse
            attended[i] = result.astype(BF16)
            lengths[0, i] = inverse
            lengths[1, i] = largest
            o_send[block_of(i)] = refolded(result, fold, (spaces, n // fold, lanes))

    o_recv[me] = o_send[me]
    start_exchange(o_send, o_recv, o_sems)
    finish_exchange(g_ref, g_recv, g_sems)

    @pl.loop(0, cycle // group)
    def _(back):
        base = (cycle // group - 1 - back) * group
        grads, mixers, deltas, limits = [], [], [], []
        for m in range(group):
            i = base + m
            query = query_of(i)
            grad_out = unfolded(g_recv[block_of(i)], fold)
            inverse = lengths[0, i]
            delta = jnp.sum(grad_out * attended[i].astype(F32), axis=0, keepdims=True) * inverse
            grad_out = jnp.concatenate([none, grad_out * inverse], axis=0)
            grads.append(grad_out.astype(BF16))
            mixers += [query.T.astype(BF16), grad_out.T.astype(BF16)]
            deltas.append(delta)
            limits.append(lengths[1, i])
        mixer = jnp.concatenate(mixers, axis=0)

        def pull(j, carry, members):
            carry = list(carry)
            key_block, turned_block = keys_of(j), turned_keys[j]
            mixed = []
            for m in members:
                factor = jnp.exp(maxima[slot(base + m, j)] - limits[m])
                block = weights[slot(base + m, j)].astype(F32) * factor
                grad = (block * (dot(key_block, grads[m]) - deltas[m])).astype(BF16)
                mixed += [grad, block.astype(BF16)]
                carry[m] = carry[m] + dot(turned_block, grad)
            total[j] += dot(jnp.concatenate(mixed, axis=1), mixer[2 * members[0] * q_tok :])
            return tuple(carry)

        carry = (jnp.zeros((lanes, q_tok), F32),) * group
        carry = lax.fori_loop(0, base, lambda j, carry: pull(j, carry, range(group)), carry)
        for m in range(group):
            carry = pull(base + m, carry, range(m, group))
        for m in range(group):
            i = base + m
            dq_ref[block_of(i)] = refolded(
                carry[m][:HEAD] * scale, fold, (spaces, n // fold, lanes)
            )
            for step in range(1, parts):
                piece = total[i, step * q_tok : (step + 1) * q_tok]
                keys[step, block_of(i)] = piece.astype(BF16).reshape(spaces, n, lanes)
                part_copy(step, i).start()

    @pl.loop(0, cycle)
    def _(back):
        j = cycle - 1 - back
        summed = total[j, :q_tok]
        for step in range(1, parts):
            part_copy(step, j).wait()
            summed += arrived[step - 1, block_of(j)].reshape(q_tok, lanes).astype(F32)
        dkv_ref[block_of(j)] = summed.astype(BF16).reshape(spaces, n, lanes)

    finish_exchange(o_send, o_recv, o_sems)


def attention(qkv, g, frames, frame_part, fold, parts):
    cycle, spaces = lax.axis_size("tm"), lax.axis_size("space")
    count, some, lanes = g.shape
    n = some * fold
    q_tok, k_tok = spaces * n, parts * spaces * n
    pairs = cycle * (cycle + 1) // 2
    folded = (count, some, lanes)
    others = max(parts - 1, 1)
    return pl.pallas_call(
        functools.partial(attention_kernel, frames, frame_part, fold, HEAD ** (-0.5)),
        out_shape=(
            jax.ShapeDtypeStruct(folded, BF16),
            jax.ShapeDtypeStruct((count, n, lanes), BF16),
            jax.ShapeDtypeStruct(folded, BF16),
        ),
        in_specs=[VMEM, VMEM],
        out_specs=(VMEM, VMEM, VMEM),
        scratch_shapes=[
            pltpu.VMEM(folded, BF16),
            pltpu.VMEM(folded, BF16),
            pltpu.VMEM((parts, count, n, lanes), BF16),
            pltpu.VMEM((cycle, lanes, k_tok), BF16),
            pltpu.VMEM((cycle, k_tok, lanes), F32),
            pltpu.VMEM((others, count, n, lanes), BF16),
            pltpu.VMEM((pairs, k_tok, q_tok), BF16),
            pltpu.VMEM((pairs, 1, q_tok), F32),
            pltpu.VMEM((2, cycle, 1, q_tok), F32),
            pltpu.VMEM((cycle, HEAD, q_tok), BF16),
            [pltpu.SemaphoreType.DMA((count,))] * 2,
            [pltpu.SemaphoreType.DMA((count,))] * 2,
            pltpu.SemaphoreType.DMA((2, others)),
            pltpu.SemaphoreType.DMA((2, others, cycle)),
        ],
        compiler_params=pltpu.CompilerParams(
            vmem_limit_bytes=62 * 1024 * 1024, collective_id=1, has_side_effects=True
        ),
        cost_estimate=pl.CostEstimate(
            flops=12 * pairs * k_tok * q_tok * lanes,
            bytes_accessed=4 * count * n * lanes,
            transcendentals=pairs * k_tok * q_tok,
        ),
    )(qkv, g)


def tokens_of(part, parts, tokens, frames):
    size = tokens // frames // parts
    return [pl.ds((frame * parts + part) * size, size) for frame in range(frames)]


def pack(send, arrays, parts, spaces, frames, fold):
    tokens, width = arrays[0].shape

    for head in range(width // HEAD):
        for part in range(parts):
            lanes = pl.ds(head * HEAD, HEAD)
            q, k, v = (
                jnp.concatenate(
                    [ref[rows, lanes] for rows in tokens_of(part, parts, tokens, frames)], axis=0
                )
                for ref in arrays
            )
            to = (head // spaces * parts + part) * spaces + head % spaces
            n = tokens // parts
            send[to, :n] = jnp.concatenate([k, v], axis=1)
            size = n // fold
            pieces = [q[m * size : (m + 1) * size] for m in range(fold)]
            if fold == 1:
                pieces.append(jnp.zeros_like(q))
            send[to, n:] = jnp.concatenate(pieces, axis=1)


def unpack(recv, arrays, parts, spaces, frames, fold):
    tokens, width = arrays[0].shape
    n = tokens // parts
    size = n // fold

    for pair in range(width // HEAD // 2):
        for part in range(parts):
            found = []
            for head in (2 * pair, 2 * pair + 1):
                block = recv[(head // spaces * parts + part) * spaces + head % spaces]
                q = [block[n:, m * HEAD : (m + 1) * HEAD] for m in range(fold)]
                found.append((jnp.concatenate(q, axis=0), block[:n, :HEAD], block[:n, HEAD:]))
            for ref, low, high in zip(arrays, *found):
                both = jnp.concatenate([low, high], axis=1)
                share = n // frames
                for frame, rows in enumerate(tokens_of(part, parts, tokens, frames)):
                    ref[rows, pl.ds(pair * 2 * HEAD, 2 * HEAD)] = both[
                        frame * share : (frame + 1) * share
                    ]


def conv_kernel(adjoint, parts, fold, field_ref, taps_ref, *rest):
    if adjoint:
        mixing, *arrays, out_ref, landed_ref, recv_ref, send_ref = rest[:8]
    else:
        send_ref, out_ref, *arrays, recv_ref = rest[:6]
    around, shifted, total, near_sems, sems = rest[-5:]
    step = pl.program_id(0)
    frames, cols, rows, channels = field_ref.shape
    lag, row = step // 3, step % 3
    count, me = everyone()
    cycle, spaces = lax.axis_size("tm"), lax.axis_size("space")
    position, column = lax.axis_index("tm"), lax.axis_index("space")
    here, far, first = (0, frames, 0) if adjoint else (2, 0, frames - 2)
    ahead = lax.rem(position + (cycle - 1 if adjoint else 1), cycle)
    right, left = lax.rem(column + 1, spaces), lax.rem(column + spaces - 1, spaces)

    def halo():
        edge = pl.ds(first, 2)
        beyond = pl.ds(far, 2)
        within = pl.ds(here, frames)
        plan = (
            (field_ref.at[edge], around.at[beyond, pl.ds(1, cols)], (ahead, column)),
            (field_ref.at[:, cols - 1], around.at[within, 0], (position, right)),
            (field_ref.at[:, 0], around.at[within, cols + 1], (position, left)),
            (field_ref.at[edge, cols - 1], around.at[beyond, 0], (ahead, right)),
            (field_ref.at[edge, 0], around.at[beyond, cols + 1], (ahead, left)),
        )
        return [
            remote(source, target, (near_sems.at[0, k], near_sems.at[1, k]), where)
            for k, (source, target, where) in enumerate(plan)
        ]

    @pl.when(step == 0)
    def _():
        if adjoint:
            pack(send_ref, arrays, parts, spaces, frames, fold)
        greet_everyone()
        for copy in halo():
            copy.start()
        start_exchange(send_ref, recv_ref, sems)
        recv_ref[me] = send_ref[me]
        centre = field_ref[...]
        around[here : here + frames, 1 : 1 + cols] = centre
        total[...] = centre.reshape(-1, channels).astype(F32)
        for copy in halo():
            copy.wait()
        outside = position == (cycle - 1 if adjoint else 0)
        beyond = around[far : far + 2]
        around[far : far + 2] = jnp.where(outside, jnp.zeros_like(beyond), beyond)
        for frame in range(frames + 2):
            whole = around[frame]
            flat = whole.astype(F32).reshape(-1, channels)
            place_in = lax.broadcasted_iota(jnp.int32, flat.shape, 0) % rows
            above = jnp.where(place_in == 0, 0.0, pltpu.roll(flat, 1, 0))
            below = jnp.where(place_in == rows - 1, 0.0, pltpu.roll(flat, flat.shape[0] - 1, 0))
            shifted[0, frame] = above.astype(BF16).reshape(whole.shape)
            shifted[1, frame] = whole
            shifted[2, frame] = below.astype(BF16).reshape(whole.shape)

    accum = total[...]
    for col in range(3):
        if adjoint:
            window = shifted[2 - row, pl.ds(2 - lag, frames), 2 - col : 2 - col + cols]
            sides = (((1,), (1,)), ((), ()))
        else:
            window = shifted[row, pl.ds(lag, frames), col : col + cols]
            sides = (((1,), (0,)), ((), ()))
        accum += lax.dot_general(
            window.reshape(-1, channels), taps_ref[0, col], sides, preferred_element_type=F32
        )
    total[...] = accum

    @pl.when(step == pl.num_programs(0) - 1)
    def _():
        result = total[...].astype(BF16)
        if adjoint:
            result = lax.dot_general(
                result, mixing[...], (((1,), (1,)), ((), ())), preferred_element_type=F32
            ).astype(BF16)
        out_ref[...] = result
        finish_exchange(send_ref, recv_ref, sems)
        if adjoint:
            landed_ref[...] = recv_ref[...]
        else:
            unpack(recv_ref, arrays, parts, spaces, frames, fold)


def convolve(field, taps, parts, fold, out_proj=None, arrays=None, send=None):
    frames, cols, rows, channels = field.shape
    tokens = frames * cols * rows
    count = lax.axis_size("tm") * lax.axis_size("space")
    adjoint = out_proj is not None
    n = tokens // parts
    travelling = (count, n + n // fold, 2 * HEAD)
    specs = [
        pl.BlockSpec(field.shape, lambda g: (0, 0, 0, 0)),
        pl.BlockSpec((1, 3, channels, channels), lambda g: (g, 0, 0, 0)),
    ]
    operands = [field, taps.reshape(9, 3, channels, channels)]
    buffer = pltpu.VMEM(travelling, BF16)
    if adjoint:
        operands += [out_proj, *arrays]
        specs += [pl.BlockSpec(x.shape, lambda g: (0, 0)) for x in (out_proj, *arrays)]
        shapes = [(tokens, out_proj.shape[0]), travelling]
    else:
        operands += [send]
        specs += [pl.BlockSpec(send.shape, lambda g: (0, 0, 0))]
        width = n * count // tokens * HEAD
        shapes = [(tokens, channels)] + [(tokens, width)] * 3
    around = (frames + 2, cols + 2, rows, channels)
    return pl.pallas_call(
        functools.partial(conv_kernel, adjoint, parts, fold),
        grid=(9,),
        out_shape=tuple(jax.ShapeDtypeStruct(shape, BF16) for shape in shapes),
        in_specs=specs,
        out_specs=tuple(
            pl.BlockSpec(shape, lambda g, rank=len(shape): (0,) * rank) for shape in shapes
        ),
        scratch_shapes=[buffer] * (2 if adjoint else 1)
        + [
            pltpu.VMEM(around, BF16),
            pltpu.VMEM((3,) + around, BF16),
            pltpu.VMEM((tokens, channels), F32),
            pltpu.SemaphoreType.DMA((2, 5)),
            [pltpu.SemaphoreType.DMA((count,))] * 2,
        ],
        compiler_params=pltpu.CompilerParams(
            vmem_limit_bytes=40 * 1024 * 1024,
            collective_id=0 if adjoint else 2,
            has_side_effects=True,
        ),
        cost_estimate=pl.CostEstimate(
            flops=54 * tokens * channels * channels,
            bytes_accessed=54 * channels * channels,
            transcendentals=0,
        ),
    )(*operands)


def by_head(array, parts, spaces):
    frames, rows, cols, width = array.shape
    array = array.reshape(frames, parts, rows // parts, cols, -1, spaces, HEAD)
    array = array.transpose(4, 1, 5, 0, 2, 3, 6)
    return array.reshape(-1, frames * (rows // parts) * cols, HEAD)


def by_token(array, shape, parts, spaces):
    frames, rows, cols, width = shape
    array = array.reshape(-1, parts, spaces, frames, rows // parts, cols, HEAD)
    return array.transpose(3, 1, 4, 5, 0, 2, 6).reshape(shape)


def folded(array, fold):
    size = array.shape[1] // fold
    pieces = [array[:, k * size : (k + 1) * size] for k in range(fold)]
    if fold == 1:
        pieces.append(jnp.zeros_like(array))
    return jnp.concatenate(pieces, axis=2)


def opened(array, fold):
    return jnp.concatenate([array[:, :, k * HEAD : (k + 1) * HEAD] for k in range(fold)], axis=1)


def shards(queries, key_rows, value_rows, out_proj, conv_taps, cotangent):
    frames, rows, cols, width = shape = queries.shape
    channels = out_proj.shape[1]
    cycle, spaces = lax.axis_size("tm"), lax.axis_size("space")
    parts = cycle * spaces // (width // HEAD)
    frame_part = rows // parts * cols
    n = frames * frame_part
    fold = 2 if n % 32 == 0 else 1

    arrays = [x.reshape(-1, width) for x in (queries, key_rows, value_rows)]
    turned = cotangent.transpose(0, 2, 1, 3)
    grad_attended, qkv = convolve(turned, conv_taps, parts, fold, out_proj, arrays)
    grad_attended = grad_attended.reshape(frames, cols, rows, width).transpose(0, 2, 1, 3)
    g = folded(by_head(grad_attended, parts, spaces), fold)
    dq, dkv, attended = attention(qkv, g, frames, frame_part, fold, parts)

    attended = by_token(opened(attended, fold), shape, parts, spaces)
    attended = attended.transpose(0, 2, 1, 3).reshape(-1, width)
    projected = dot(attended, out_proj).astype(BF16).reshape(frames, cols, rows, channels)
    back = jnp.concatenate([dkv, dq], axis=1)
    conv_output, *grads = convolve(projected, conv_taps, parts, fold, send=back)
    conv_output = conv_output.reshape(frames, cols, rows, channels).transpose(0, 2, 1, 3)
    return (conv_output, *(x.reshape(shape) for x in grads))


def solution(mesh):
    tokens = P("tm", None, "space", None)
    return jax.shard_map(
        shards,
        mesh=mesh,
        in_specs=(tokens, tokens, tokens, P(), P(), tokens),
        out_specs=(tokens, tokens, tokens, tokens),
        check_vma=False,
    )
```

```python
import functools

import jax
import jax.numpy as jnp
from jax import lax
from jax.experimental import pallas as pl
from jax.experimental.pallas import tpu as pltpu
from jax.sharding import PartitionSpec as P

HEAD = 64
NEGATIVE = -1e30
F32 = jnp.float32
BF16 = jnp.bfloat16
MESH = pl.DeviceIdType.MESH
VMEM = pl.BlockSpec(memory_space=pltpu.VMEM)


def dot(left, right):
    return jnp.dot(left, right, preferred_element_type=F32)


def everyone():
    cycle, spaces = lax.axis_size("tm"), lax.axis_size("space")
    me = lax.axis_index("tm") * spaces + lax.axis_index("space")
    return cycle * spaces, me


def place(index):
    spaces = lax.axis_size("space")
    return (index // spaces, lax.rem(index, spaces))


def greet_everyone():
    count, me = everyone()
    barrier = pltpu.get_barrier_semaphore()

    @pl.loop(1, count)
    def _(i):
        pl.semaphore_signal(
            barrier, inc=1, device_id=place(lax.rem(me + i, count)), device_id_type=MESH
        )

    pl.semaphore_wait(barrier, count - 1)


def remote(source, target, sems, where):
    return pltpu.make_async_remote_copy(
        src_ref=source,
        dst_ref=target,
        send_sem=sems[0],
        recv_sem=sems[1],
        device_id=where,
        device_id_type=MESH,
    )


def block_copy(send, recv, sems, i, arriving):
    count, me = everyone()
    other = lax.rem(me - i + count, count) if arriving else lax.rem(me + i, count)
    landing = other if arriving else me
    pair = (sems[0].at[i], sems[1].at[i])
    return remote(send.at[other], recv.at[landing], pair, place(other))


def start_exchange(send, recv, sems):
    count, me = everyone()

    @pl.loop(1, count)
    def _(i):
        block_copy(send, recv, sems, i, False).start()


def finish_exchange(send, recv, sems):
    count, me = everyone()

    @pl.loop(1, count)
    def _(i):
        block_copy(send, recv, sems, i, True).wait_recv()

    @pl.loop(1, count)
    def _(i):
        block_copy(send, recv, sems, i, False).wait_send()


def unfolded(block, fold):
    turned = block.reshape(-1, block.shape[-1]).astype(F32).T
    return jnp.concatenate([turned[k * HEAD : (k + 1) * HEAD] for k in range(fold)], axis=1)


def refolded(turned, fold, shape):
    width = turned.shape[1] // fold
    pieces = [turned[:, k * width : (k + 1) * width] for k in range(fold)]
    if fold == 1:
        pieces.append(jnp.zeros_like(pieces[0]))
    return jnp.concatenate(pieces, axis=0).T.astype(BF16).reshape(shape)


def attention_kernel(
    frames,
    frame_part,
    fold,
    scale,
    qkv_ref,
    g_ref,
    dq_ref,
    dkv_ref,
    o_recv,
    g_recv,
    o_send,
    keys,
    turned_keys,
    total,
    arrived,
    weights,
    maxima,
    lengths,
    attended,
    g_sems,
    o_sems,
    key_sems,
    part_sems,
):
    cycle, spaces = lax.axis_size("tm"), lax.axis_size("space")
    count, me = everyone()
    parts, _, n, lanes = keys.shape
    q_tok, k_tok = spaces * n, parts * spaces * n
    position, column = lax.axis_index("tm"), lax.axis_index("space")
    part = lax.rem(position, parts)
    group = 4 if cycle % 4 == 0 and cycle < 16 else 2 if cycle % 2 == 0 else 1

    def sibling(step):
        return (position - part + lax.rem(part + step + parts, parts), column)

    def key_copy(step):
        pair = (key_sems.at[0, step - 1], key_sems.at[1, step - 1])
        return remote(keys.at[0], keys.at[step], pair, sibling(step))

    def part_copy(step, j):
        pair = (part_sems.at[0, step - 1, j], part_sems.at[1, step - 1, j])
        rows = pl.ds(j * spaces, spaces)
        return remote(
            keys.at[step, rows], arrived.at[step - 1, rows], pair, sibling(-step)
        )

    def block_of(j):
        return pl.ds(j * spaces, spaces)

    def keys_of(j):
        return keys[:, block_of(j)].reshape(k_tok, lanes)

    @pl.loop(0, cycle)
    def _(j):
        keys[0, block_of(j)] = qkv_ref[block_of(j), :n]

    greet_everyone()
    for step in range(1, parts):
        key_copy(step).start()
    start_exchange(g_ref, g_recv, g_sems)
    g_recv[me] = g_ref[me]

    key_token = lax.broadcasted_iota(jnp.int32, (k_tok, q_tok), 0) % n
    query_token = lax.broadcasted_iota(jnp.int32, (k_tok, q_tok), 1)
    query_token = query_token // (q_tok // fold) * (n // fold) + query_token % (n // fold)
    visible = key_token // frame_part <= query_token // frame_part
    for step in range(1, parts):
        key_copy(step).wait()

    @pl.loop(0, cycle)
    def _(j):
        turned_keys[j] = keys_of(j).astype(F32).T.astype(BF16)
        total[j] = jnp.zeros((k_tok, lanes), F32)

    none = jnp.zeros((HEAD, q_tok), F32)

    def query_of(i):
        return jnp.concatenate([unfolded(qkv_ref[block_of(i), n:], fold) * scale, none], axis=0)

    def slot(i, j):
        return i * (i + 1) // 2 + j

    @pl.loop(0, cycle // group)
    def _(several):
        base = several * group
        queries = [query_of(base + m).astype(BF16) for m in range(group)]

        def weigh(j, carry, members, masked=None):
            carry = list(carry)
            key_block, turned_block = keys_of(j), turned_keys[j]
            for m in members:
                accum, length, largest = carry[m]
                scores = dot(key_block, queries[m])
                if m == masked:
                    scores = jnp.where(visible, scores, NEGATIVE)
                above = jnp.maximum(largest, jnp.max(scores, axis=0, keepdims=True))
                factor = jnp.exp(largest - above)
                block = jnp.exp(scores - above)
                length = length * factor + jnp.sum(block, axis=0, keepdims=True)
                block = block.astype(BF16)
                weights[slot(base + m, j)] = block
                maxima[slot(base + m, j)] = above
                carry[m] = (accum * factor + dot(turned_block, block), length, above)
            return tuple(carry)

        carry = (
            (
                jnp.zeros((lanes, q_tok), F32),
                jnp.zeros((1, q_tok), F32),
                jnp.full((1, q_tok), NEGATIVE, F32),
            ),
        ) * group
        for m in range(group):
            carry = weigh(base + m, carry, range(m, group), m)
        carry = lax.fori_loop(0, base, lambda j, carry: weigh(j, carry, range(group)), carry)
        for m, (accum, length, largest) in enumerate(carry):
            i = base + m
            inverse = 1.0 / length
            result = accum[HEAD:] * inverse
            attended[i] = result.astype(BF16)
            lengths[0, i] = inverse
            lengths[1, i] = largest
            o_send[block_of(i)] = refolded(result, fold, (spaces, n // fold, lanes))

    o_recv[me] = o_send[me]
    start_exchange(o_send, o_recv, o_sems)
    finish_exchange(g_ref, g_recv, g_sems)

    @pl.loop(0, cycle // group)
    def _(back):
        base = (cycle // group - 1 - back) * group
        grads, mixers, deltas, limits = [], [], [], []
        for m in range(group):
            i = base + m
            query = query_of(i)
            grad_out = unfolded(g_recv[block_of(i)], fold)
            inverse = lengths[0, i]
            delta = jnp.sum(grad_out * attended[i].astype(F32), axis=0, keepdims=True) * inverse
            grad_out = jnp.concatenate([none, grad_out * inverse], axis=0)
            grads.append(grad_out.astype(BF16))
            mixers += [query.T.astype(BF16), grad_out.T.astype(BF16)]
            deltas.append(delta)
            limits.append(lengths[1, i])
        mixer = jnp.concatenate(mixers, axis=0)

        def pull(j, carry, members):
            carry = list(carry)
            key_block, turned_block = keys_of(j), turned_keys[j]
            mixed = []
            for m in members:
                factor = jnp.exp(maxima[slot(base + m, j)] - limits[m])
                block = weights[slot(base + m, j)].astype(F32) * factor
                grad = (block * (dot(key_block, grads[m]) - deltas[m])).astype(BF16)
                mixed += [grad, block.astype(BF16)]
                carry[m] = carry[m] + dot(turned_block, grad)
            total[j] += dot(jnp.concatenate(mixed, axis=1), mixer[2 * members[0] * q_tok :])
            return tuple(carry)

        carry = (jnp.zeros((lanes, q_tok), F32),) * group
        carry = lax.fori_loop(0, base, lambda j, carry: pull(j, carry, range(group)), carry)
        for m in range(group):
            carry = pull(base + m, carry, range(m, group))
        for m in range(group):
            i = base + m
            dq_ref[block_of(i)] = refolded(
                carry[m][:HEAD] * scale, fold, (spaces, n // fold, lanes)
            )
            for step in range(1, parts):
                piece = total[i, step * q_tok : (step + 1) * q_tok]
                keys[step, block_of(i)] = piece.astype(BF16).reshape(spaces, n, lanes)
                part_copy(step, i).start()

    @pl.loop(0, cycle)
    def _(back):
        j = cycle - 1 - back
        summed = total[j, :q_tok]
        for step in range(1, parts):
            part_copy(step, j).wait()
            summed += arrived[step - 1, block_of(j)].reshape(q_tok, lanes).astype(F32)
        dkv_ref[block_of(j)] = summed.astype(BF16).reshape(spaces, n, lanes)

    finish_exchange(o_send, o_recv, o_sems)


def attention(qkv, g, frames, frame_part, fold, parts):
    cycle, spaces = lax.axis_size("tm"), lax.axis_size("space")
    count, some, lanes = g.shape
    n = some * fold
    q_tok, k_tok = spaces * n, parts * spaces * n
    pairs = cycle * (cycle + 1) // 2
    folded = (count, some, lanes)
    others = max(parts - 1, 1)
    return pl.pallas_call(
        functools.partial(attention_kernel, frames, frame_part, fold, HEAD ** (-0.5)),
        out_shape=(
            jax.ShapeDtypeStruct(folded, BF16),
            jax.ShapeDtypeStruct((count, n, lanes), BF16),
            jax.ShapeDtypeStruct(folded, BF16),
        ),
        in_specs=[VMEM, VMEM],
        out_specs=(VMEM, VMEM, VMEM),
        scratch_shapes=[
            pltpu.VMEM(folded, BF16),
            pltpu.VMEM(folded, BF16),
            pltpu.VMEM((parts, count, n, lanes), BF16),
            pltpu.VMEM((cycle, lanes, k_tok), BF16),
            pltpu.VMEM((cycle, k_tok, lanes), F32),
            pltpu.VMEM((others, count, n, lanes), BF16),
            pltpu.VMEM((pairs, k_tok, q_tok), BF16),
            pltpu.VMEM((pairs, 1, q_tok), F32),
            pltpu.VMEM((2, cycle, 1, q_tok), F32),
            pltpu.VMEM((cycle, HEAD, q_tok), BF16),
            [pltpu.SemaphoreType.DMA((count,))] * 2,
            [pltpu.SemaphoreType.DMA((count,))] * 2,
            pltpu.SemaphoreType.DMA((2, others)),
            pltpu.SemaphoreType.DMA((2, others, cycle)),
        ],
        compiler_params=pltpu.CompilerParams(
            vmem_limit_bytes=62 * 1024 * 1024, collective_id=1, has_side_effects=True
        ),
        cost_estimate=pl.CostEstimate(
            flops=12 * pairs * k_tok * q_tok * lanes,
            bytes_accessed=4 * count * n * lanes,
            transcendentals=pairs * k_tok * q_tok,
        ),
    )(qkv, g)


def tokens_of(part, parts, tokens, lines):
    size = tokens // lines // parts
    return [pl.ds((line * parts + part) * size, size) for line in range(lines)]


def piece_of(ref, head, part, parts, lines):
    lanes = pl.ds(head * HEAD, HEAD)
    places = tokens_of(part, parts, ref.shape[0], lines)
    return jnp.concatenate([ref[rows, lanes] for rows in places], axis=0)


def folded(piece, fold):
    size = piece.shape[0] // fold
    pieces = [piece[m * size : (m + 1) * size] for m in range(fold)]
    if fold == 1:
        pieces.append(jnp.zeros_like(piece))
    return jnp.concatenate(pieces, axis=1)


def opened(block, fold):
    return jnp.concatenate([block[:, m * HEAD : (m + 1) * HEAD] for m in range(fold)], axis=0)


def device_of(head, part, parts, spaces):
    return (head // spaces * parts + part) * spaces + head % spaces


def pack(send, arrays, parts, spaces, lines, fold):
    tokens, width = arrays[0].shape
    for head in range(width // HEAD):
        for part in range(parts):
            q, k, v = (piece_of(ref, head, part, parts, lines) for ref in arrays)
            to, n = device_of(head, part, parts, spaces), tokens // parts
            send[to, :n] = jnp.concatenate([k, v], axis=1)
            send[to, n:] = folded(q, fold)


def pack_one(send, array, parts, spaces, lines, fold):
    for head in range(array.shape[1] // HEAD):
        for part in range(parts):
            piece = piece_of(array, head, part, parts, lines)
            send[device_of(head, part, parts, spaces)] = folded(piece, fold)


def unpack(arrays, parts, spaces, lines, found_of):
    tokens, width = arrays[0].shape
    share = tokens // parts // lines
    for pair in range(width // HEAD // 2):
        for part in range(parts):
            found = [
                found_of(device_of(head, part, parts, spaces)) for head in (2 * pair, 2 * pair + 1)
            ]
            for ref, low, high in zip(arrays, *found):
                both = jnp.concatenate([low, high], axis=1)
                for line, rows in enumerate(tokens_of(part, parts, tokens, lines)):
                    lanes = pl.ds(pair * 2 * HEAD, 2 * HEAD)
                    ref[rows, lanes] = both[line * share : (line + 1) * share]


def conv_kernel(adjoint, shape, parts, fold, first_ref, taps_ref, mixing, *rest):
    if adjoint:
        field_ref = first_ref
        *arrays, out_ref, landed_ref, recv_ref, send_ref, wide = rest[:8]
    else:
        send_ref, out_ref, *arrays, recv_ref, wide, field_ref = rest[:8]
    around, shifted, total, near_sems, sems = rest[-5:]
    frames, cols, rows, channels = shape
    lines = frames * cols
    step = pl.program_id(0)
    lag, row = step // 3, step % 3
    count, me = everyone()
    cycle, spaces = lax.axis_size("tm"), lax.axis_size("space")
    position, column = lax.axis_index("tm"), lax.axis_index("space")
    here, far, first = (0, frames, 0) if adjoint else (2, 0, frames - 2)
    ahead = lax.rem(position + (cycle - 1 if adjoint else 1), cycle)
    right, left = lax.rem(column + 1, spaces), lax.rem(column + spaces - 1, spaces)

    def halo():
        edge = pl.ds(first, 2)
        beyond = pl.ds(far, 2)
        within = pl.ds(here, frames)
        plan = (
            (field_ref.at[edge], around.at[beyond, pl.ds(1, cols)], (ahead, column)),
            (field_ref.at[:, cols - 1], around.at[within, 0], (position, right)),
            (field_ref.at[:, 0], around.at[within, cols + 1], (position, left)),
            (field_ref.at[edge, cols - 1], around.at[beyond, 0], (ahead, right)),
            (field_ref.at[edge, 0], around.at[beyond, cols + 1], (ahead, left)),
        )
        return [
            remote(source, target, (near_sems.at[0, k], near_sems.at[1, k]), where)
            for k, (source, target, where) in enumerate(plan)
        ]

    @pl.when(step == 0)
    def _():
        if adjoint:
            pack(send_ref, arrays, parts, spaces, lines, fold)
        else:
            unpack([wide], parts, spaces, lines, lambda at: (opened(first_ref[at], fold),))
            field_ref[...] = dot(wide[...], mixing[...]).astype(BF16).reshape(shape)
        greet_everyone()
        for copy in halo():
            copy.start()
        start_exchange(send_ref, recv_ref, sems)
        recv_ref[me] = send_ref[me]
        centre = field_ref[...]
        around[here : here + frames, 1 : 1 + cols] = centre
        total[...] = centre.reshape(-1, channels).astype(F32)
        for copy in halo():
            copy.wait()
        outside = position == (cycle - 1 if adjoint else 0)
        beyond = around[far : far + 2]
        around[far : far + 2] = jnp.where(outside, jnp.zeros_like(beyond), beyond)
        for frame in range(frames + 2):
            whole = around[frame]
            flat = whole.astype(F32).reshape(-1, channels)
            place_in = lax.broadcasted_iota(jnp.int32, flat.shape, 0) % rows
            above = jnp.where(place_in == 0, 0.0, pltpu.roll(flat, 1, 0))
            below = jnp.where(place_in == rows - 1, 0.0, pltpu.roll(flat, flat.shape[0] - 1, 0))
            shifted[0, frame] = above.astype(BF16).reshape(whole.shape)
            shifted[1, frame] = whole
            shifted[2, frame] = below.astype(BF16).reshape(whole.shape)

    accum = total[...]
    for col in range(3):
        if adjoint:
            window = shifted[2 - row, pl.ds(2 - lag, frames), 2 - col : 2 - col + cols]
            sides = (((1,), (1,)), ((), ()))
        else:
            window = shifted[row, pl.ds(lag, frames), col : col + cols]
            sides = (((1,), (0,)), ((), ()))
        accum += lax.dot_general(
            window.reshape(-1, channels), taps_ref[0, col], sides, preferred_element_type=F32
        )
    total[...] = accum

    @pl.when(step == pl.num_programs(0) - 1)
    def _():
        result = total[...].astype(BF16)
        if adjoint:
            wide[...] = lax.dot_general(
                result, mixing[...], (((1,), (1,)), ((), ())), preferred_element_type=F32
            ).astype(BF16)
            pack_one(out_ref, wide, parts, spaces, lines, fold)
        else:
            out_ref[...] = result
        finish_exchange(send_ref, recv_ref, sems)
        if adjoint:
            landed_ref[...] = recv_ref[...]
        else:
            n = lines * rows // parts

            def found_of(at):
                block = recv_ref[at]
                return opened(block[n:], fold), block[:n, :HEAD], block[:n, HEAD:]

            unpack(arrays, parts, spaces, lines, found_of)


def convolve(shape, first, taps, out_proj, parts, fold, arrays=None, send=None):
    frames, cols, rows, channels = shape
    tokens = frames * cols * rows
    count = lax.axis_size("tm") * lax.axis_size("space")
    adjoint = arrays is not None
    n, width = tokens // parts, out_proj.shape[0]
    travelling = (count, n + n // fold, 2 * HEAD)
    operands = [first, taps.reshape(9, 3, channels, channels), out_proj]
    operands += arrays if adjoint else [send]

    def whole(shape):
        return pl.BlockSpec(shape, lambda g: (0,) * len(shape))

    specs = [whole(x.shape) for x in operands]
    specs[1] = pl.BlockSpec((1, 3, channels, channels), lambda g: (g, 0, 0, 0))
    buffer, wide = pltpu.VMEM(travelling, BF16), pltpu.VMEM((tokens, width), BF16)
    if adjoint:
        shapes = [(count, n // fold, 2 * HEAD), travelling]
        buffers = [buffer, buffer, wide]
    else:
        shapes = [(tokens, channels)] + [(tokens, width)] * 3
        buffers = [buffer, wide, pltpu.VMEM(shape, BF16)]
    around = (frames + 2, cols + 2, rows, channels)
    return pl.pallas_call(
        functools.partial(conv_kernel, adjoint, shape, parts, fold),
        grid=(9,),
        out_shape=tuple(jax.ShapeDtypeStruct(x, BF16) for x in shapes),
        in_specs=specs,
        out_specs=tuple(whole(shape) for shape in shapes),
        scratch_shapes=buffers
        + [
            pltpu.VMEM(around, BF16),
            pltpu.VMEM((3,) + around, BF16),
            pltpu.VMEM((tokens, channels), F32),
            pltpu.SemaphoreType.DMA((2, 5)),
            [pltpu.SemaphoreType.DMA((count,))] * 2,
        ],
        compiler_params=pltpu.CompilerParams(
            vmem_limit_bytes=40 * 1024 * 1024,
            collective_id=0 if adjoint else 2,
            has_side_effects=True,
        ),
        cost_estimate=pl.CostEstimate(
            flops=54 * tokens * channels * channels,
            bytes_accessed=54 * channels * channels,
            transcendentals=0,
        ),
    )(*operands)


def shards(queries, key_rows, value_rows, out_proj, conv_taps, cotangent):
    frames, rows, cols, width = queries.shape
    shape = (frames, cols, rows, out_proj.shape[1])
    cycle, spaces = lax.axis_size("tm"), lax.axis_size("space")
    parts = cycle * spaces // (width // HEAD)
    frame_part = rows // parts * cols
    n = frames * frame_part
    fold = 2 if n % 32 == 0 else 1

    def turned(array):
        return array.transpose(0, 2, 1, 3)

    arrays = [turned(x).reshape(-1, width) for x in (queries, key_rows, value_rows)]
    g, qkv = convolve(shape, turned(cotangent), conv_taps, out_proj, parts, fold, arrays=arrays)
    dq, dkv, attended = attention(qkv, g, frames, frame_part, fold, parts)
    back = jnp.concatenate([dkv, dq], axis=1)
    outs = convolve(shape, attended, conv_taps, out_proj, parts, fold, send=back)
    return tuple(turned(x.reshape(frames, cols, rows, -1)) for x in outs)


def solution(mesh):
    tokens = P("tm", None, "space", None)
    return jax.shard_map(
        shards,
        mesh=mesh,
        in_specs=(tokens, tokens, tokens, P(), P(), tokens),
        out_specs=(tokens, tokens, tokens, tokens),
        check_vma=False,
    )
```

```python
import functools

import jax
import jax.numpy as jnp
from jax import lax
from jax.experimental import pallas as pl
from jax.experimental.pallas import tpu as pltpu
from jax.sharding import PartitionSpec as P

HEAD = 64
NEGATIVE = -1e30
F32 = jnp.float32
BF16 = jnp.bfloat16
MESH = pl.DeviceIdType.MESH
VMEM = pl.BlockSpec(memory_space=pltpu.VMEM)


def dot(left, right):
    return jnp.dot(left, right, preferred_element_type=F32)


def everyone():
    cycle, spaces = lax.axis_size("tm"), lax.axis_size("space")
    me = lax.axis_index("tm") * spaces + lax.axis_index("space")
    return cycle * spaces, me


def place(index):
    spaces = lax.axis_size("space")
    return (index // spaces, lax.rem(index, spaces))


def greet_everyone():
    count, me = everyone()
    barrier = pltpu.get_barrier_semaphore()

    @pl.loop(1, count)
    def _(i):
        pl.semaphore_signal(
            barrier, inc=1, device_id=place(lax.rem(me + i, count)), device_id_type=MESH
        )

    pl.semaphore_wait(barrier, count - 1)


def remote(source, target, sems, where):
    return pltpu.make_async_remote_copy(
        src_ref=source,
        dst_ref=target,
        send_sem=sems[0],
        recv_sem=sems[1],
        device_id=where,
        device_id_type=MESH,
    )


def block_copy(send, recv, sems, i, arriving):
    count, me = everyone()
    other = lax.rem(me - i + count, count) if arriving else lax.rem(me + i, count)
    landing = other if arriving else me
    pair = (sems[0].at[i], sems[1].at[i])
    return remote(send.at[other], recv.at[landing], pair, place(other))


def start_exchange(send, recv, sems):
    count, me = everyone()

    @pl.loop(1, count)
    def _(i):
        block_copy(send, recv, sems, i, False).start()


def finish_exchange(send, recv, sems):
    count, me = everyone()

    @pl.loop(1, count)
    def _(i):
        block_copy(send, recv, sems, i, True).wait_recv()

    @pl.loop(1, count)
    def _(i):
        block_copy(send, recv, sems, i, False).wait_send()


def tokens_of(part, parts, tokens, lines):
    size = tokens // lines // parts
    return [pl.ds((line * parts + part) * size, size) for line in range(lines)]


def piece_of(ref, head, part, parts, lines):
    lanes = pl.ds(head * HEAD, HEAD)
    places = tokens_of(part, parts, ref.shape[0], lines)
    return jnp.concatenate([ref[rows, lanes] for rows in places], axis=0)


def folded(piece, fold):
    size = piece.shape[0] // fold
    pieces = [piece[m * size : (m + 1) * size] for m in range(fold)]
    if fold == 1:
        pieces.append(jnp.zeros_like(piece))
    return jnp.concatenate(pieces, axis=1)


def opened(block, fold):
    return jnp.concatenate([block[:, m * HEAD : (m + 1) * HEAD] for m in range(fold)], axis=0)


def device_of(head, part, parts, spaces):
    return (head // spaces * parts + part) * spaces + head % spaces


def pack(send, arrays, parts, spaces, lines, fold):
    tokens, width = arrays[0].shape
    for head in range(width // HEAD):
        for part in range(parts):
            q, k, v = (piece_of(ref, head, part, parts, lines) for ref in arrays)
            to, n = device_of(head, part, parts, spaces), tokens // parts
            send[to, :n] = jnp.concatenate([k, v], axis=1)
            send[to, n:] = folded(q, fold)


def pack_one(send, array, parts, spaces, lines, fold):
    for head in range(array.shape[1] // HEAD):
        for part in range(parts):
            piece = piece_of(array, head, part, parts, lines)
            send[device_of(head, part, parts, spaces)] = folded(piece, fold)


def unpack(arrays, parts, spaces, lines, found_of):
    tokens, width = arrays[0].shape
    share = tokens // parts // lines
    for pair in range(width // HEAD // 2):
        for part in range(parts):
            found = [
                found_of(device_of(head, part, parts, spaces)) for head in (2 * pair, 2 * pair + 1)
            ]
            for ref, low, high in zip(arrays, *found):
                both = jnp.concatenate([low, high], axis=1)
                for line, rows in enumerate(tokens_of(part, parts, tokens, lines)):
                    lanes = pl.ds(pair * 2 * HEAD, 2 * HEAD)
                    ref[rows, lanes] = both[line * share : (line + 1) * share]


def halo_copies(adjoint, field_ref, around, near_sems):
    frames, cols = field_ref.shape[:2]
    cycle, spaces = lax.axis_size("tm"), lax.axis_size("space")
    position, column = lax.axis_index("tm"), lax.axis_index("space")
    here, far, first = (0, frames, 0) if adjoint else (2, 0, frames - 2)
    ahead = lax.rem(position + (cycle - 1 if adjoint else 1), cycle)
    right, left = lax.rem(column + 1, spaces), lax.rem(column + spaces - 1, spaces)
    edge, beyond, within = pl.ds(first, 2), pl.ds(far, 2), pl.ds(here, frames)
    plan = (
        (field_ref.at[edge], around.at[beyond, pl.ds(1, cols)], (ahead, column)),
        (field_ref.at[:, cols - 1], around.at[within, 0], (position, right)),
        (field_ref.at[:, 0], around.at[within, cols + 1], (position, left)),
        (field_ref.at[edge, cols - 1], around.at[beyond, 0], (ahead, right)),
        (field_ref.at[edge, 0], around.at[beyond, cols + 1], (ahead, left)),
    )
    return [
        remote(source, target, (near_sems.at[0, k], near_sems.at[1, k]), where)
        for k, (source, target, where) in enumerate(plan)
    ]


def finish_halo(adjoint, field_ref, around, near_sems):
    frames = field_ref.shape[0]
    for copy in halo_copies(adjoint, field_ref, around, near_sems):
        copy.wait()
    edge = lax.axis_size("tm") - 1 if adjoint else 0
    beyond = pl.ds(frames if adjoint else 0, 2)
    outside = lax.axis_index("tm") == edge
    around[beyond] = jnp.where(outside, jnp.zeros_like(around[beyond]), around[beyond])


def unfolded(block, fold):
    turned = block.reshape(-1, block.shape[-1]).astype(F32).T
    return jnp.concatenate([turned[k * HEAD : (k + 1) * HEAD] for k in range(fold)], axis=1)


def refolded(turned, fold, shape):
    width = turned.shape[1] // fold
    pieces = [turned[:, k * width : (k + 1) * width] for k in range(fold)]
    if fold == 1:
        pieces.append(jnp.zeros_like(pieces[0]))
    return jnp.concatenate(pieces, axis=0).T.astype(BF16).reshape(shape)


def attention_kernel(
    frames,
    frame_part,
    fold,
    scale,
    qkv_ref,
    g_ref,
    mixing,
    dq_ref,
    dkv_ref,
    around_ref,
    o_recv,
    wide,
    field,
    around,
    near_sems,
    g_recv,
    o_send,
    keys,
    turned_keys,
    total,
    arrived,
    weights,
    maxima,
    lengths,
    attended,
    g_sems,
    o_sems,
    key_sems,
    part_sems,
):
    cycle, spaces = lax.axis_size("tm"), lax.axis_size("space")
    count, me = everyone()
    parts, _, n, lanes = keys.shape
    q_tok, k_tok = spaces * n, parts * spaces * n
    position, column = lax.axis_index("tm"), lax.axis_index("space")
    part = lax.rem(position, parts)
    group = 4 if cycle % 4 == 0 and cycle < 16 else 1

    def sibling(step):
        return (position - part + lax.rem(part + step + parts, parts), column)

    def key_copy(step):
        pair = (key_sems.at[0, step - 1], key_sems.at[1, step - 1])
        return remote(keys.at[0], keys.at[step], pair, sibling(step))

    def part_copy(step, j):
        pair = (part_sems.at[0, step - 1, j], part_sems.at[1, step - 1, j])
        rows = pl.ds(j * spaces, spaces)
        return remote(
            keys.at[step, rows], arrived.at[step - 1, rows], pair, sibling(-step)
        )

    def block_of(j):
        return pl.ds(j * spaces, spaces)

    def keys_of(j):
        return keys[:, block_of(j)].reshape(k_tok, lanes)

    @pl.loop(0, cycle)
    def _(j):
        keys[0, block_of(j)] = qkv_ref[block_of(j), :n]

    greet_everyone()
    for step in range(1, parts):
        key_copy(step).start()
    start_exchange(g_ref, g_recv, g_sems)
    g_recv[me] = g_ref[me]

    key_token = lax.broadcasted_iota(jnp.int32, (k_tok, q_tok), 0) % n
    query_token = lax.broadcasted_iota(jnp.int32, (k_tok, q_tok), 1)
    query_token = query_token // (q_tok // fold) * (n // fold) + query_token % (n // fold)
    visible = key_token // frame_part <= query_token // frame_part
    for step in range(1, parts):
        key_copy(step).wait()

    @pl.loop(0, cycle)
    def _(j):
        turned_keys[j] = keys_of(j).astype(F32).T.astype(BF16)
        total[j] = jnp.zeros((k_tok, lanes), F32)

    none = jnp.zeros((HEAD, q_tok), F32)

    def query_of(i):
        return jnp.concatenate([unfolded(qkv_ref[block_of(i), n:], fold) * scale, none], axis=0)

    def slot(i, j):
        return i * (i + 1) // 2 + j

    @pl.loop(0, cycle // group)
    def _(several):
        base = several * group
        queries = [query_of(base + m).astype(BF16) for m in range(group)]

        def weigh(j, carry, members, masked=None):
            carry = list(carry)
            key_block, turned_block = keys_of(j), turned_keys[j]
            for m in members:
                accum, length, largest = carry[m]
                scores = dot(key_block, queries[m])
                if m == masked:
                    scores = jnp.where(visible, scores, NEGATIVE)
                above = jnp.maximum(largest, jnp.max(scores, axis=0, keepdims=True))
                factor = jnp.exp(largest - above)
                block = jnp.exp(scores - above)
                length = length * factor + jnp.sum(block, axis=0, keepdims=True)
                block = block.astype(BF16)
                weights[slot(base + m, j)] = block
                maxima[slot(base + m, j)] = above
                carry[m] = (accum * factor + dot(turned_block, block), length, above)
            return tuple(carry)

        carry = (
            (
                jnp.zeros((lanes, q_tok), F32),
                jnp.zeros((1, q_tok), F32),
                jnp.full((1, q_tok), NEGATIVE, F32),
            ),
        ) * group
        for m in range(group):
            carry = weigh(base + m, carry, range(m, group), m)
        carry = lax.fori_loop(0, base, lambda j, carry: weigh(j, carry, range(group)), carry)
        for m, (accum, length, largest) in enumerate(carry):
            i = base + m
            inverse = 1.0 / length
            result = accum[HEAD:] * inverse
            attended[i] = result.astype(BF16)
            lengths[0, i] = inverse
            lengths[1, i] = largest
            o_send[block_of(i)] = refolded(result, fold, (spaces, n // fold, lanes))

    o_recv[me] = o_send[me]
    start_exchange(o_send, o_recv, o_sems)
    finish_exchange(g_ref, g_recv, g_sems)

    @pl.loop(0, cycle // group)
    def _(back):
        base = (cycle // group - 1 - back) * group

        @pl.when(back == cycle // group - 1)
        def _():
            finish_exchange(o_send, o_recv, o_sems)
            lines = field.shape[0] * field.shape[1]
            unpack([wide], parts, spaces, lines, lambda at: (opened(o_recv[at], fold),))
            field[...] = dot(wide[...], mixing[...]).astype(BF16).reshape(field.shape)
            for copy in halo_copies(False, field, around, near_sems):
                copy.start()

        grads, mixers, deltas, limits = [], [], [], []
        for m in range(group):
            i = base + m
            query = query_of(i)
            grad_out = unfolded(g_recv[block_of(i)], fold)
            inverse = lengths[0, i]
            delta = jnp.sum(grad_out * attended[i].astype(F32), axis=0, keepdims=True) * inverse
            grad_out = jnp.concatenate([none, grad_out * inverse], axis=0)
            grads.append(grad_out.astype(BF16))
            mixers += [query.T.astype(BF16), grad_out.T.astype(BF16)]
            deltas.append(delta)
            limits.append(lengths[1, i])
        mixer = jnp.concatenate(mixers, axis=0)

        def pull(j, carry, members):
            carry = list(carry)
            key_block, turned_block = keys_of(j), turned_keys[j]
            mixed = []
            for m in members:
                factor = jnp.exp(maxima[slot(base + m, j)] - limits[m])
                block = weights[slot(base + m, j)].astype(F32) * factor
                grad = (block * (dot(key_block, grads[m]) - deltas[m])).astype(BF16)
                mixed += [grad, block.astype(BF16)]
                carry[m] = carry[m] + dot(turned_block, grad)
            total[j] += dot(jnp.concatenate(mixed, axis=1), mixer[2 * members[0] * q_tok :])
            return tuple(carry)

        carry = (jnp.zeros((lanes, q_tok), F32),) * group
        carry = lax.fori_loop(0, base, lambda j, carry: pull(j, carry, range(group)), carry)
        for m in range(group):
            carry = pull(base + m, carry, range(m, group))
        for m in range(group):
            i = base + m
            dq_ref[block_of(i)] = refolded(
                carry[m][:HEAD] * scale, fold, (spaces, n // fold, lanes)
            )
            for step in range(1, parts):
                piece = total[i, step * q_tok : (step + 1) * q_tok]
                keys[step, block_of(i)] = piece.astype(BF16).reshape(spaces, n, lanes)
                part_copy(step, i).start()

    @pl.loop(0, cycle)
    def _(back):
        j = cycle - 1 - back
        summed = total[j, :q_tok]
        for step in range(1, parts):
            part_copy(step, j).wait()
            summed += arrived[step - 1, block_of(j)].reshape(q_tok, lanes).astype(F32)
        dkv_ref[block_of(j)] = summed.astype(BF16).reshape(spaces, n, lanes)

    around[2 : 2 + field.shape[0], 1 : 1 + field.shape[1]] = field[...]
    finish_halo(False, field, around, near_sems)
    around_ref[...] = around[...]


def attention(qkv, g, out_proj, shape, frame_part, fold, parts):
    cycle, spaces = lax.axis_size("tm"), lax.axis_size("space")
    count, some, lanes = g.shape
    n = some * fold
    q_tok, k_tok = spaces * n, parts * spaces * n
    pairs = cycle * (cycle + 1) // 2
    folded = (count, some, lanes)
    frames, cols, rows, channels = shape
    surrounded = (frames + 2, cols + 2, rows, channels)
    others = max(parts - 1, 1)
    return pl.pallas_call(
        functools.partial(attention_kernel, frames, frame_part, fold, HEAD ** (-0.5)),
        out_shape=(
            jax.ShapeDtypeStruct(folded, BF16),
            jax.ShapeDtypeStruct((count, n, lanes), BF16),
            jax.ShapeDtypeStruct(surrounded, BF16),
        ),
        in_specs=[VMEM, VMEM, VMEM],
        out_specs=(VMEM, VMEM, VMEM),
        scratch_shapes=[
            pltpu.VMEM(folded, BF16),
            pltpu.VMEM((frames * cols * rows, out_proj.shape[0]), BF16),
            pltpu.VMEM(shape, BF16),
            pltpu.VMEM(surrounded, BF16),
            pltpu.SemaphoreType.DMA((2, 5)),
            pltpu.VMEM(folded, BF16),
            pltpu.VMEM(folded, BF16),
            pltpu.VMEM((parts, count, n, lanes), BF16),
            pltpu.VMEM((cycle, lanes, k_tok), BF16),
            pltpu.VMEM((cycle, k_tok, lanes), F32),
            pltpu.VMEM((others, count, n, lanes), BF16),
            pltpu.VMEM((pairs, k_tok, q_tok), BF16),
            pltpu.VMEM((pairs, 1, q_tok), F32),
            pltpu.VMEM((2, cycle, 1, q_tok), F32),
            pltpu.VMEM((cycle, HEAD, q_tok), BF16),
            [pltpu.SemaphoreType.DMA((count,))] * 2,
            [pltpu.SemaphoreType.DMA((count,))] * 2,
            pltpu.SemaphoreType.DMA((2, others)),
            pltpu.SemaphoreType.DMA((2, others, cycle)),
        ],
        compiler_params=pltpu.CompilerParams(
            vmem_limit_bytes=62 * 1024 * 1024, collective_id=1, has_side_effects=True
        ),
        cost_estimate=pl.CostEstimate(
            flops=12 * pairs * k_tok * q_tok * lanes,
            bytes_accessed=4 * count * n * lanes,
            transcendentals=pairs * k_tok * q_tok,
        ),
    )(qkv, g, out_proj)


def conv_kernel(adjoint, shape, parts, fold, first_ref, taps_ref, mixing, *rest):
    if adjoint:
        field_ref = first_ref
        *arrays, out_ref, landed_ref, recv_ref, send_ref, wide = rest[:8]
    else:
        send_ref, out_ref, *arrays, recv_ref = rest[:6]
    around, shifted, total, near_sems, sems = rest[-5:]
    if not adjoint:
        around = first_ref
    frames, cols, rows, channels = shape
    lines = frames * cols
    step = pl.program_id(0)
    lag, row = step // 3, step % 3
    count, me = everyone()
    cycle, spaces = lax.axis_size("tm"), lax.axis_size("space")
    position, column = lax.axis_index("tm"), lax.axis_index("space")
    here = 0 if adjoint else 2
    centre_of = (pl.ds(here, frames), pl.ds(1, cols))

    @pl.when(step == 0)
    def _():
        if adjoint:
            pack(send_ref, arrays, parts, spaces, lines, fold)
        greet_everyone()
        if adjoint:
            for copy in halo_copies(True, field_ref, around, near_sems):
                copy.start()
        start_exchange(send_ref, recv_ref, sems)
        recv_ref[me] = send_ref[me]
        if adjoint:
            around[centre_of] = field_ref[...]
            finish_halo(True, field_ref, around, near_sems)
        total[...] = around[centre_of].reshape(-1, channels).astype(F32)
        for frame in range(frames + 2):
            whole = around[frame]
            flat = whole.astype(F32).reshape(-1, channels)
            place_in = lax.broadcasted_iota(jnp.int32, flat.shape, 0) % rows
            above = jnp.where(place_in == 0, 0.0, pltpu.roll(flat, 1, 0))
            below = jnp.where(place_in == rows - 1, 0.0, pltpu.roll(flat, flat.shape[0] - 1, 0))
            shifted[0, frame] = above.astype(BF16).reshape(whole.shape)
            shifted[1, frame] = whole
            shifted[2, frame] = below.astype(BF16).reshape(whole.shape)

    accum = total[...]
    for col in range(3):
        if adjoint:
            window = shifted[2 - row, pl.ds(2 - lag, frames), 2 - col : 2 - col + cols]
            sides = (((1,), (1,)), ((), ()))
        else:
            window = shifted[row, pl.ds(lag, frames), col : col + cols]
            sides = (((1,), (0,)), ((), ()))
        accum += lax.dot_general(
            window.reshape(-1, channels), taps_ref[0, col], sides, preferred_element_type=F32
        )
    total[...] = accum

    @pl.when(step == pl.num_programs(0) - 1)
    def _():
        result = total[...].astype(BF16)
        if adjoint:
            wide[...] = lax.dot_general(
                result, mixing[...], (((1,), (1,)), ((), ())), preferred_element_type=F32
            ).astype(BF16)
            pack_one(out_ref, wide, parts, spaces, lines, fold)
        else:
            out_ref[...] = result
        finish_exchange(send_ref, recv_ref, sems)
        if adjoint:
            landed_ref[...] = recv_ref[...]
        else:
            n = lines * rows // parts

            def found_of(at):
                block = recv_ref[at]
                return opened(block[n:], fold), block[:n, :HEAD], block[:n, HEAD:]

            unpack(arrays, parts, spaces, lines, found_of)


def convolve(shape, first, taps, out_proj, parts, fold, arrays=None, send=None):
    frames, cols, rows, channels = shape
    tokens = frames * cols * rows
    count = lax.axis_size("tm") * lax.axis_size("space")
    adjoint = arrays is not None
    n, width = tokens // parts, out_proj.shape[0]
    travelling = (count, n + n // fold, 2 * HEAD)
    operands = [first, taps.reshape(9, 3, channels, channels), out_proj]
    operands += arrays if adjoint else [send]

    def whole(shape):
        return pl.BlockSpec(shape, lambda g: (0,) * len(shape))

    specs = [whole(x.shape) for x in operands]
    specs[1] = pl.BlockSpec((1, 3, channels, channels), lambda g: (g, 0, 0, 0))
    buffer, wide = pltpu.VMEM(travelling, BF16), pltpu.VMEM((tokens, width), BF16)
    if adjoint:
        shapes = [(count, n // fold, 2 * HEAD), travelling]
        buffers = [buffer, buffer, wide]
    else:
        shapes = [(tokens, channels)] + [(tokens, width)] * 3
        buffers = [buffer]
    around = (frames + 2, cols + 2, rows, channels)
    return pl.pallas_call(
        functools.partial(conv_kernel, adjoint, shape, parts, fold),
        grid=(9,),
        out_shape=tuple(jax.ShapeDtypeStruct(x, BF16) for x in shapes),
        in_specs=specs,
        out_specs=tuple(whole(shape) for shape in shapes),
        scratch_shapes=buffers
        + [
            pltpu.VMEM(around, BF16),
            pltpu.VMEM((3,) + around, BF16),
            pltpu.VMEM((tokens, channels), F32),
            pltpu.SemaphoreType.DMA((2, 5)),
            [pltpu.SemaphoreType.DMA((count,))] * 2,
        ],
        compiler_params=pltpu.CompilerParams(
            vmem_limit_bytes=40 * 1024 * 1024,
            collective_id=0 if adjoint else 2,
            has_side_effects=True,
        ),
        cost_estimate=pl.CostEstimate(
            flops=54 * tokens * channels * channels,
            bytes_accessed=54 * channels * channels,
            transcendentals=0,
        ),
    )(*operands)


def shards(queries, key_rows, value_rows, out_proj, conv_taps, cotangent):
    frames, rows, cols, width = queries.shape
    shape = (frames, cols, rows, out_proj.shape[1])
    cycle, spaces = lax.axis_size("tm"), lax.axis_size("space")
    parts = cycle * spaces // (width // HEAD)
    frame_part = rows // parts * cols
    n = frames * frame_part
    fold = 2 if n % 32 == 0 else 1

    def turned(array):
        return array.transpose(0, 2, 1, 3)

    arrays = [turned(x).reshape(-1, width) for x in (queries, key_rows, value_rows)]
    g, qkv = convolve(shape, turned(cotangent), conv_taps, out_proj, parts, fold, arrays=arrays)
    dq, dkv, projected = attention(qkv, g, out_proj, shape, frame_part, fold, parts)
    back = jnp.concatenate([dkv, dq], axis=1)
    outs = convolve(shape, projected, conv_taps, out_proj, parts, fold, send=back)
    return tuple(turned(x.reshape(frames, cols, rows, -1)) for x in outs)


def solution(mesh):
    tokens = P("tm", None, "space", None)
    return jax.shard_map(
        shards,
        mesh=mesh,
        in_specs=(tokens, tokens, tokens, P(), P(), tokens),
        out_specs=(tokens, tokens, tokens, tokens),
        check_vma=False,
    )
```
